32 devices in a mesh: row: 4 (over x, core), col: 2 (over y), env: 4 (over z).
Axes of the slice: x: 2, y: 2, z: 4, core: 2. Of those that a mesh axis runs over, the one named last changes fastest.
Arguments:
- corner: bfloat16 [4, 2, 1024, 1024], P('row', 'col'), may hold values from -0.1875 to 0.1875
- top_edge: bfloat16 [4, 2, 1024, 32768], P('row', 'col', 'env'), may hold values from -0.03125 to 0.03125
- half_system: bfloat16 [4, 2, 1024, 32768], P('row', 'col', 'env'), may hold values from -0.03125 to 0.03125
- values: float32 [4, 2, 1024], P('row', 'col'), may hold values from 0.5 to 4
- cotangent: bfloat16 [4, 2, 1024, 1024], P('row', 'col'), may hold values from -32 to 32
- parity: int32 [4, 2, 4, 8], P('row', 'col'), may hold values 0 or 1
Outputs:
- grad_corner: bfloat16 [4, 2, 1024, 1024], P('row', 'col', 'env')
- grad_edge: bfloat16 [4, 2, 1024, 32768], P('row', 'col', 'env')
- grad_half: bfloat16 [4, 2, 1024, 32768], P('row', 'col', 'env')
- grad_values: float32 [4, 2, 1024], P('row', 'col', 'env')
The draws below stay inside these ranges and needn't reach their ends.
Inputs may be any that keep to these rules, and one draw needn't show every extreme that they name: `parity`: each entry is the Z2 charge of one block of 128 environment indices.
All inputs are finite; a program needn't handle non-finite values.
Results may differ from the reference program's by a relative error of at most 0.0058.
Values may be sent and summed in bfloat16 or wider, within the bound.
No kernel may reach another device: no remote copies, remote signals or barrier semaphores. Data moves between devices by JAX's collectives and lax.ppermute only.
A program may use at most 192 MiB of HBM per device.

```python
import math
import jax
import jax.numpy as jnp
from jax import lax

CHI = 1024
HALF = 32
BLK = 128
NBLK = 8
ROWS = 4
COLS = 2


def touch_ends(drawn, own_key, smallest, high):
    extent = drawn.shape
    index_at = [jax.random.randint(jax.random.fold_in(own_key, axis), (), 0, extent[axis]) for axis in range(len(extent))]
    drawn = drawn.at[tuple(index_at)].set(smallest)
    longest = extent.index(max(extent))
    index_at[longest] = (index_at[longest] + 1) % extent[longest]
    return drawn.at[tuple(index_at)].set(high)


def block_scale(own_key, shape, pieces, smallest, high):
    def one(dim, shards_of):
        heights = jax.random.uniform(jax.random.fold_in(jax.random.fold_in(own_key, 6), dim), (shards_of,), jnp.float32, smallest / len(pieces), high / len(pieces))
        return jnp.repeat(jnp.exp(heights), shape[dim] // shards_of).reshape((-1,) + (1,) * (len(shape) - dim - 1))

    level = one(*pieces[0])
    for cut in pieces[1:]:
        level = level * one(*cut)
    return level


def bell_draw(key, shape, width, limit, shards=(), held_as=jnp.bfloat16):
    level = block_scale(key, shape, shards, -0.22, 0.18) if shards else 1.0
    entries = jax.random.normal(key, shape, jnp.float32) * width * level
    return jnp.minimum(jnp.maximum(entries, -limit), limit).astype(held_as)


def setup_inputs(seed: int = 0) -> dict:
    streams_of = jax.random.split(jax.random.key(seed), 7)
    corner = bell_draw(streams_of[0], (ROWS, COLS, CHI, CHI), CHI ** -0.5, 0.1875, ((0, 4), (1, 2)))
    top_edge = bell_draw(streams_of[1], (ROWS, COLS, CHI, HALF * CHI), (CHI * HALF) ** -0.5, 0.03125, ((0, 4), (1, 2), (2, 4)))
    half_system = bell_draw(streams_of[2], (ROWS, COLS, CHI, CHI * HALF), (CHI * HALF) ** -0.5, 0.03125, ((0, 4), (1, 2), (2, 4)))
    values = jnp.clip(jnp.exp(math.log(4.0) - 2.0794415 * jax.random.uniform(streams_of[3], (ROWS, COLS, CHI), jnp.float32) ** block_scale(streams_of[3], (ROWS, COLS, CHI), ((0, 4), (1, 2)), -0.2, 0.2)), 0.5, 4.0)
    cotangent = bell_draw(streams_of[4], (ROWS, COLS, CHI, CHI), (HALF ** 0.5), 32.0, ((0, 4), (1, 2)))
    parity = touch_ends((jax.random.randint(streams_of[5], (ROWS, COLS, 4, NBLK), 0, 2) < 1).astype(jnp.int32), jax.random.fold_in(streams_of[5], 1), 0, 1)
    return {"corner": corner, "top_edge": top_edge, "half_system": half_system, "values": values, "cotangent": cotangent, "parity": parity}


def charge_masks(parity_site):
    charges = jnp.repeat(parity_site, BLK, axis=1)
    corner_mask = charges[0][:, None] == charges[1][None, :]
    out_mask = charges[2][:, None] == charges[3][None, :]
    return corner_mask, out_mask


def one_site(near_corner, top_edge, half_system, values, cotangent, parity_site):
    corner_mask, out_mask = charge_masks(parity_site)
    masked = jnp.where(corner_mask, near_corner, jnp.zeros_like(near_corner)).astype(jnp.float32)
    lower_half = half_system.reshape(CHI, CHI, HALF).astype(jnp.float32)
    absorbed = jnp.einsum("ab,iak->ibk", masked, lower_half, precision=lax.Precision.HIGHEST).astype(jnp.bfloat16)
    absorbed = lax.optimization_barrier(absorbed)
    flat = absorbed.reshape(CHI, CHI * HALF).astype(jnp.float32)
    edge_mat = top_edge.reshape(CHI * HALF, CHI).astype(jnp.float32)
    weight = values ** -0.5
    grad_new = jnp.where(out_mask, weight[:, None] * cotangent.astype(jnp.float32), jnp.float32(0.0)).astype(jnp.bfloat16)
    grad_new = lax.optimization_barrier(grad_new)
    grad_newf = grad_new.astype(jnp.float32)
    grad_edge = jnp.dot(flat.T, grad_newf, precision=lax.Precision.HIGHEST)
    grad_full = jnp.dot(grad_newf, edge_mat.T, precision=lax.Precision.HIGHEST)
    pair_sums = jnp.sum(flat * grad_full, axis=1)
    grad_values = -0.5 * pair_sums / values
    grad_back = lax.optimization_barrier(grad_full.astype(jnp.bfloat16))
    grad_back = grad_back.astype(jnp.float32).reshape(CHI, CHI, HALF)
    grad_half = jnp.einsum("ab,ibk->iak", masked, grad_back, precision=lax.Precision.HIGHEST)
    grad_half = grad_half.astype(jnp.bfloat16).reshape(CHI, CHI * HALF)
    summed = jnp.einsum("iak,ibk->ab", lower_half, grad_back, precision=lax.Precision.HIGHEST)
    grad_corner = jnp.where(corner_mask, summed, jnp.float32(0.0)).astype(jnp.bfloat16)
    grad_edge = grad_edge.astype(jnp.bfloat16).reshape(CHI, HALF * CHI)
    return grad_corner, grad_edge, grad_half, grad_values


def reference(corner, top_edge, half_system, values, cotangent, parity):
    corner_grid = [[None] * COLS for row_index in range(ROWS)]
    edge_grid = [[None] * COLS for row_index in range(ROWS)]
    half_grid = [[None] * COLS for row_index in range(ROWS)]
    value_grid = [[None] * COLS for row_index in range(ROWS)]
    for row_index in range(ROWS):
        for col_index in range(COLS):
            left_col = (col_index - 1) % COLS
            below_row = (row_index + 1) % ROWS
            results = one_site(corner[row_index, left_col], top_edge[row_index, col_index],
                               half_system[below_row, col_index], values[row_index, col_index],
                               cotangent[row_index, col_index], parity[row_index, col_index])
            corner_grid[row_index][left_col] = results[0]
            edge_grid[row_index][col_index] = results[1]
            half_grid[below_row][col_index] = results[2]
            value_grid[row_index][col_index] = results[3]

    def stacked(grid):
        return jnp.stack([jnp.stack(row_list) for row_list in grid])

    return stacked(corner_grid), stacked(edge_grid), stacked(half_grid), stacked(value_grid)
```

```python
import functools

import jax
import jax.numpy as jnp
from jax import lax
from jax.experimental import pallas as pl
from jax.experimental.pallas import tpu as pltpu
from jax.sharding import PartitionSpec as P

CHI = 1024
HALF = 32
BLK = 128

FULL_CHUNKS = (4, 12, 16)
EDGE_CHUNKS = (4, 6, 6, 6, 4, 3, 2, 1)

MIB = 1 << 20
F32 = jnp.float32
BF16 = jnp.bfloat16


def passed_along(x, axis, by):
    size = lax.axis_size(axis)
    return lax.ppermute(x, axis, [(i, (i + by) % size) for i in range(size)])


def swapped(x, d):
    return lax.ppermute(x, "env", [(i, i ^ d) for i in range(lax.axis_size("env"))])


def nn(a, b):
    return jnp.dot(a, b, preferred_element_type=F32)


def nt(a, b):
    return lax.dot_general(a, b, (((1,), (1,)), ((), ())), preferred_element_type=F32)


ANYWHERE = pl.BlockSpec(memory_space=pl.ANY)


def params(mib):
    return pltpu.CompilerParams(
        vmem_limit_bytes=mib * MIB, dimension_semantics=("arbitrary",)
    )


def cost(count, rows, moved):
    return pl.CostEstimate(
        flops=2 * count * rows * CHI * CHI, bytes_accessed=moved, transcendentals=0
    )


def full_chunk(me, top_edge, grad_new, first, count, after):
    rows = top_edge.shape[0]
    n = CHI // rows
    n_after = len(after)

    def kernel(me_ref, t_ref, *refs):
        g_refs, outs = refs[:n], refs[n + n_after:]
        t = t_ref[...]
        for g_ref, out in zip(g_refs, outs):
            out[0] = nt(t, g_ref[...]).astype(BF16)

    def grad_spec(d):
        return pl.BlockSpec((rows, CHI), lambda k, me: (me[0] ^ d, 0))

    return pl.pallas_call(
        kernel,
        grid_spec=pltpu.PrefetchScalarGridSpec(
            num_scalar_prefetch=1,
            grid=(count,),
            in_specs=[pl.BlockSpec((rows, CHI), lambda k, me: (0, first + k))]
            + [grad_spec(d) for d in range(n)] + [ANYWHERE] * n_after,
            out_specs=[pl.BlockSpec((1, rows, rows), lambda k, me: (k, 0, 0))] * n,
        ),
        out_shape=[jax.ShapeDtypeStruct((count, rows, rows), BF16)] * n,
        compiler_params=params(24),
        cost_estimate=cost(count, rows, 4 * count * rows * CHI),
        name="grad_full",
    )(me, top_edge, *[grad_new] * n, *after)


def absorbed_chunk(me, lower, corner_t, first, count, after):
    rows = lower.shape[2]
    n = CHI // rows
    n_after = len(after)

    def kernel(me_ref, l_ref, *refs):
        c_refs, outs = refs[:n], refs[n + n_after:]
        low = l_ref[0]
        for c_ref, out in zip(c_refs, outs):
            out[0] = nn(c_ref[...], low).astype(BF16)

    def corner_spec(d):
        return pl.BlockSpec((rows, CHI), lambda k, me: (me[0] ^ d, 0))

    return pl.pallas_call(
        kernel,
        grid_spec=pltpu.PrefetchScalarGridSpec(
            num_scalar_prefetch=1,
            grid=(count,),
            in_specs=[pl.BlockSpec((1, CHI, rows), lambda k, me: (first + k, 0, 0))]
            + [corner_spec(d) for d in range(n)] + [ANYWHERE] * n_after,
            out_specs=[pl.BlockSpec((1, rows, rows), lambda k, me: (k, 0, 0))] * n,
        ),
        out_shape=[jax.ShapeDtypeStruct((count, rows, rows), BF16)] * n,
        compiler_params=params(24),
        cost_estimate=cost(count, rows, 4 * count * rows * CHI),
        name="absorbed",
    )(me, lower, *[corner_t] * n, *after)


def half_chunk(me, blocks, lower, corner, held, first, count):
    rows = lower.shape[2]
    n = CHI // rows
    step = 2 if count % 2 == 0 and first % 2 == 0 else 1
    has_held = held is not None

    def kernel(me_ref, l_ref, *refs):
        f_refs, c_refs = refs[:n], refs[n:2 * n]
        half_ref, corner_ref, pair_ref = refs[-3:]

        @pl.when(pl.program_id(0) == 0)
        def _():
            corner_ref[...] = jnp.zeros_like(corner_ref)
            pair_ref[...] = jnp.zeros_like(pair_ref)

        for j in range(step):
            total = nn(c_refs[0][...], f_refs[0][j])
            for d in range(1, n):
                total += nn(c_refs[d][...], f_refs[d][j])
            half_ref[j] = total.astype(BF16)
            part = total * l_ref[j].astype(F32)
            pair_ref[...] += jnp.sum(part.reshape(CHI // 8, 8, rows), axis=0)
        low = jnp.concatenate([l_ref[j] for j in range(step)], axis=1)
        for d in range(n):
            full = jnp.concatenate([f_refs[d][j] for j in range(step)], axis=1)
            place = pl.ds(pl.multiple_of((me_ref[0] ^ d) * rows, rows), rows)
            corner_ref[:, place] += nt(low, full)

    def corner_spec(d):
        return pl.BlockSpec((CHI, rows), lambda k, me: (0, me[0] ^ d))

    operands = [me, lower, *blocks, *[corner] * n] + ([held] if has_held else [])
    return pl.pallas_call(
        kernel,
        grid_spec=pltpu.PrefetchScalarGridSpec(
            num_scalar_prefetch=1,
            grid=(count // step,),
            in_specs=[pl.BlockSpec((step, CHI, rows), lambda k, me: (first // step + k, 0, 0))]
            + [pl.BlockSpec((step, rows, rows), lambda k, me: (k, 0, 0))] * n
            + [corner_spec(d) for d in range(n)] + [ANYWHERE] * has_held,
            out_specs=[
                pl.BlockSpec((step, CHI, rows), lambda k, me: (first // step + k, 0, 0)),
                pl.BlockSpec((CHI, CHI), lambda k, me: (0, 0)),
                pl.BlockSpec((8, rows), lambda k, me: (0, 0)),
            ],
        ),
        out_shape=[
            jax.ShapeDtypeStruct(lower.shape, BF16),
            jax.ShapeDtypeStruct((CHI, CHI), F32),
            jax.ShapeDtypeStruct((8, rows), F32),
        ],
        input_output_aliases={len(operands) - 1: 0} if has_held else {},
        compiler_params=params(40),
        cost_estimate=cost(2 * count, rows, 6 * count * rows * CHI),
        name="grad_half",
    )(*operands)


def edge_chunk(me, blocks, grad_new, held, first, count):
    rows = blocks[0].shape[1]
    n = CHI // rows
    has_held = held is not None

    def kernel(me_ref, *refs):
        a_refs, g_refs, out = refs[:n], refs[n:2 * n], refs[-1]
        total = nn(a_refs[0][0], g_refs[0][...])
        for d in range(1, n):
            total += nn(a_refs[d][0], g_refs[d][...])
        out[...] = total.astype(BF16)

    def grad_spec(d):
        return pl.BlockSpec((rows, CHI), lambda k, me: (me[0] ^ d, 0))

    operands = [me, *blocks, *[grad_new] * n] + ([held] if has_held else [])
    return pl.pallas_call(
        kernel,
        grid_spec=pltpu.PrefetchScalarGridSpec(
            num_scalar_prefetch=1,
            grid=(count,),
            in_specs=[pl.BlockSpec((1, rows, rows), lambda k, me: (k, 0, 0))] * n
            + [grad_spec(d) for d in range(n)] + [ANYWHERE] * has_held,
            out_specs=pl.BlockSpec((rows, CHI), lambda k, me: (0, first + k)),
        ),
        out_shape=jax.ShapeDtypeStruct((rows, HALF * CHI), BF16),
        input_output_aliases={len(operands) - 1: 0} if has_held else {},
        compiler_params=params(24),
        cost_estimate=cost(count, rows, 4 * count * rows * CHI),
        name="grad_edge",
    )(*operands)


def exchanged(blocks):
    return [blocks[0]] + [swapped(blocks[d], d) for d in range(1, len(blocks))]


def summed_rows(partial, me, rows):
    left = partial.reshape(CHI // rows, rows, CHI)
    bit = 1
    while left.shape[0] > 1:
        pairs = left.reshape(left.shape[0] // 2, 2, rows, CHI)
        own = lax.rem(lax.div(me, jnp.int32(bit)), jnp.int32(2))
        kept = lax.dynamic_index_in_dim(pairs, own, 1, keepdims=False)
        sent = lax.dynamic_index_in_dim(pairs, 1 - own, 1, keepdims=False).astype(BF16)
        left = kept + swapped(sent, bit).astype(F32)
        bit *= 2
    return left[0]


def charge_masks(parity):
    charges = jnp.repeat(parity, BLK, axis=1)
    corner_mask = charges[0][:, None] == charges[1][None, :]
    out_mask = charges[2][:, None] == charges[3][None, :]
    return corner_mask, out_mask


def chunked_shards(corner, top_edge, half_system, values, cotangent, parity):
    rows = top_edge.shape[2]
    me = lax.axis_index("env").astype(jnp.int32)
    me_arr = me.reshape(1)
    corner_mask, out_mask = charge_masks(parity[0, 0])

    grad_new = jnp.where(
        out_mask, values[0, 0][:, None] ** (-0.5) * cotangent[0, 0].astype(F32), 0.0
    ).astype(BF16)

    lower_half = passed_along(half_system[0, 0], "row", -1)
    near_corner = passed_along(corner[0, 0], "col", 1)
    near_corner = jnp.where(corner_mask, near_corner, jnp.zeros_like(near_corner))

    in_flight = []

    def waits():
        return in_flight[-2] if len(in_flight) > 1 else []

    full_parts, first = [], 0
    for count in FULL_CHUNKS:
        blocks = full_chunk(me_arr, top_edge[0, 0], grad_new, first, count, waits())
        blocks = exchanged(blocks)
        in_flight.append(blocks[1:])
        full_parts.append((first, count, blocks))
        first += count

    lower = lower_half.T.reshape(CHI, HALF, rows).transpose(1, 0, 2)
    corner_t = near_corner.T

    edge_parts, first = [], 0
    for count in EDGE_CHUNKS:
        blocks = absorbed_chunk(me_arr, lower, corner_t, first, count, waits())
        blocks = exchanged(blocks)
        in_flight.append(blocks[1:])
        edge_parts.append((first, count, blocks))
        first += count

    grad_half, corner_total, pair_total = None, 0.0, 0.0
    for first, count, blocks in full_parts:
        grad_half, corner_part, pair_part = half_chunk(
            me_arr, blocks, lower, near_corner, grad_half, first, count
        )
        corner_total = corner_total + corner_part
        pair_total = pair_total + pair_part

    own_values = lax.dynamic_slice_in_dim(values[0, 0], me * rows, rows, 0)
    grad_values = -0.5 * jnp.sum(pair_total, axis=0) / own_values

    grad_half = grad_half.transpose(1, 0, 2).reshape(CHI * HALF, rows).T
    grad_half = passed_along(grad_half, "row", 1)

    own_mask = lax.dynamic_slice_in_dim(corner_mask, me * rows, rows, 0)
    grad_corner = jnp.where(own_mask, summed_rows(corner_total, me, rows), 0.0)
    grad_corner = passed_along(grad_corner.astype(BF16), "col", -1)

    grad_edge = None
    for first, count, blocks in edge_parts:
        grad_edge = edge_chunk(me_arr, blocks, grad_new, grad_edge, first, count)

    return (
        grad_corner[None, None],
        grad_edge[None, None],
        grad_half[None, None],
        grad_values[None, None],
    )


def whole_shards(corner, top_edge, half_system, values, cotangent, parity):
    rows = top_edge.shape[2]
    row_start = lax.axis_index("env") * rows
    corner_mask, out_mask = charge_masks(parity[0, 0])
    near_corner = passed_along(corner[0, 0], "col", 1)
    near_corner = jnp.where(corner_mask, near_corner, jnp.zeros_like(near_corner))
    lower_half = passed_along(half_system[0, 0], "row", -1).reshape(rows, CHI, HALF)
    absorbed = jnp.einsum("ab,iak->ibk", near_corner, lower_half, preferred_element_type=F32)
    absorbed = absorbed.astype(BF16).reshape(rows, CHI * HALF)
    gathered = lax.all_to_all(absorbed, "env", split_axis=1, concat_axis=0, tiled=True)
    edge_mat = top_edge[0, 0].reshape(rows * HALF, CHI)
    grad_new = jnp.where(
        out_mask, values[0, 0][:, None] ** (-0.5) * cotangent[0, 0].astype(F32), 0.0
    ).astype(BF16)
    grad_edge = jnp.einsum("ij,ie->je", gathered, grad_new, preferred_element_type=F32)
    grad_edge = grad_edge.astype(BF16).reshape(rows, HALF * CHI)
    grad_full = jnp.einsum("ie,je->ij", grad_new, edge_mat, preferred_element_type=F32)
    totals = lax.psum(jnp.sum(gathered * grad_full, axis=1), "env")
    pair_sums = lax.dynamic_slice_in_dim(totals, row_start, rows, 0)
    own_values = lax.dynamic_slice_in_dim(values[0, 0], row_start, rows, 0)
    grad_values = -0.5 * pair_sums / own_values
    grad_back = lax.all_to_all(
        grad_full.astype(BF16), "env", split_axis=0, concat_axis=1, tiled=True
    ).reshape(rows, CHI, HALF)
    grad_half = jnp.einsum("ab,ibk->iak", near_corner, grad_back, preferred_element_type=F32)
    grad_half = grad_half.astype(BF16).reshape(rows, CHI * HALF)
    summed = jnp.einsum("iak,ibk->ab", lower_half, grad_back, preferred_element_type=F32)
    summed = lax.psum_scatter(summed, "env", scatter_dimension=0, tiled=True)
    own_mask = lax.dynamic_slice_in_dim(corner_mask, row_start, rows, 0)
    grad_corner = jnp.where(own_mask, summed, 0.0).astype(BF16)
    grad_corner = passed_along(grad_corner, "col", -1)
    grad_half = passed_along(grad_half, "row", 1)
    return (
        grad_corner[None, None],
        grad_edge[None, None],
        grad_half[None, None],
        grad_values[None, None],
    )


def solution(mesh):
    n = mesh.shape["env"]
    chunked = n & (n - 1) == 0 and CHI // n % BLK == 0
    return jax.shard_map(
        chunked_shards if chunked else whole_shards,
        mesh=mesh,
        in_specs=(
            P("row", "col", None, None),
            P("row", "col", "env", None),
            P("row", "col", "env", None),
            P("row", "col", None),
            P("row", "col", None, None),
            P("row", "col", None, None),
        ),
        out_specs=(
            P("row", "col", "env", None),
            P("row", "col", "env", None),
            P("row", "col", "env", None),
            P("row", "col", "env"),
        ),
        check_vma=False,
    )
```

```python
import functools

import jax
import jax.numpy as jnp
from jax import lax
from jax.experimental import pallas as pl
from jax.experimental.layout import Layout, with_layout_constraint
from jax.experimental.pallas import tpu as pltpu
from jax.sharding import PartitionSpec as P

CHI = 1024
HALF = 32
BLK = 128

FULL_CHUNKS = (4, 28)
EDGE_CHUNKS = (9, 9, 6, 4, 3, 1)
ENV = 4

MIB = 1 << 20
VMEM_MIB = 56
COST_BITS = 20
HELD_BACK = {1: 0}
ORDER = "F0 F1 f C T A0 A1 a H0 H1 R1 A2 E0 A3 M E1 R2 A4 E2 R3 A5 E3 R4 E4 E5"
F32 = jnp.float32
BF16 = jnp.bfloat16


def passed_along(x, axis, by):
    size = lax.axis_size(axis)
    return lax.ppermute(x, axis, [(i, (i + by) % size) for i in range(size)])


def swapped(x, d, rows_on=0):
    n_row, n_env = lax.axis_size("row"), lax.axis_size("env")
    if not rows_on:
        return lax.ppermute(x, "env", [(i, i ^ d) for i in range(n_env)])
    pairs = [
        (r * n_env + i, (r + rows_on) % n_row * n_env + (i ^ d))
        for r in range(n_row) for i in range(n_env)
    ]
    return lax.ppermute(x, ("row", "env"), pairs)


def corner_moved(x, by):
    n_row, n_col = lax.axis_size("row"), lax.axis_size("col")
    pairs = [
        (r * n_col + c, (r + by) % n_row * n_col + (c + by) % n_col)
        for r in range(n_row) for c in range(n_col)
    ]
    return lax.ppermute(x, ("row", "col"), pairs)


def nn(a, b):
    return jnp.dot(a, b, preferred_element_type=F32)


def nt(a, b):
    return lax.dot_general(a, b, (((1,), (1,)), ((), ())), preferred_element_type=F32)


ANYWHERE = pl.BlockSpec(memory_space=pl.ANY)


def params(dims=1):
    return pltpu.CompilerParams(
        vmem_limit_bytes=VMEM_MIB * MIB, dimension_semantics=("arbitrary",) * dims
    )


def cost(count):
    return pl.CostEstimate(
        flops=count << COST_BITS, bytes_accessed=count << (COST_BITS - 8), transcendentals=0
    )


def row_major(x):
    return with_layout_constraint(x, Layout(tuple(range(x.ndim))))


def full_chunk(me, top_edge, grad_new, ds, first, count, after):
    rows = top_edge.shape[0]
    n_out = len(ds)

    def kernel(me_ref, t_ref, *refs):
        g_refs, outs = refs[:n_out], refs[-n_out:]
        t = t_ref[...]
        for g_ref, out in zip(g_refs, outs):
            out[0] = nt(t, g_ref[...]).astype(BF16)

    def grad_spec(d):
        return pl.BlockSpec((rows, CHI), lambda k, me: (me[0] ^ d, 0))

    return pl.pallas_call(
        kernel,
        grid_spec=pltpu.PrefetchScalarGridSpec(
            num_scalar_prefetch=1,
            grid=(count,),
            in_specs=[pl.BlockSpec((rows, CHI), lambda k, me: (0, first + k))]
            + [grad_spec(d) for d in ds] + [ANYWHERE] * len(after),
            out_specs=[pl.BlockSpec((1, rows, rows), lambda k, me: (k, 0, 0))] * n_out,
        ),
        out_shape=[jax.ShapeDtypeStruct((count, rows, rows), BF16)] * n_out,
        compiler_params=params(),
        cost_estimate=cost(count),
        name="grad_full",
    )(me, top_edge, *[grad_new] * n_out, *after)


GROUP = 64


def k_major(x, after):
    rows = x.shape[0]

    def kernel(x_ref, *refs):
        turned = x_ref[...].T.reshape(GROUP, HALF, rows)
        refs[-1][...] = jnp.transpose(turned, (1, 0, 2))

    return pl.pallas_call(
        kernel,
        grid=(CHI // GROUP,),
        in_specs=[pl.BlockSpec((rows, GROUP * HALF), lambda j: (0, j))] + [ANYWHERE] * len(after),
        out_specs=pl.BlockSpec((HALF, GROUP, rows), lambda j: (0, j, 0)),
        out_shape=jax.ShapeDtypeStruct((HALF, CHI, rows), BF16),
        compiler_params=params(),
        cost_estimate=cost(1),
        name="k_major",
    )(x, *after)


def k_minor(parts, after):
    rows = parts[0].shape[2]
    n_parts = len(parts)

    def kernel(*refs):
        whole = jnp.concatenate([ref[...] for ref in refs[:n_parts]], axis=0)
        refs[-1][...] = jnp.transpose(whole, (1, 0, 2)).reshape(GROUP * HALF, rows).T

    return pl.pallas_call(
        kernel,
        grid=(CHI // GROUP,),
        in_specs=[pl.BlockSpec((x.shape[0], GROUP, rows), lambda j: (0, j, 0)) for x in parts]
        + [ANYWHERE] * len(after),
        out_specs=pl.BlockSpec((rows, GROUP * HALF), lambda j: (0, j)),
        out_shape=jax.ShapeDtypeStruct((rows, CHI * HALF), BF16),
        compiler_params=params(),
        cost_estimate=cost(1),
        name="k_minor",
    )(*parts, *after)


def held_back(arrays, after):
    n_arrays = len(arrays)
    return pl.pallas_call(
        lambda *refs: None,
        in_specs=[ANYWHERE] * (n_arrays + len(after)),
        out_specs=[ANYWHERE] * n_arrays,
        out_shape=[jax.ShapeDtypeStruct(x.shape, x.dtype) for x in arrays],
        input_output_aliases={j: j for j in range(n_arrays)},
        compiler_params=pltpu.CompilerParams(vmem_limit_bytes=VMEM_MIB * MIB),
        cost_estimate=cost(1),
        name="held_back",
    )(*arrays, *after)


def absorbed_chunk(me, lower, corner_t, ds, first, count, after):
    rows = lower.shape[2]
    n_out = len(ds)

    def kernel(me_ref, l_ref, *refs):
        c_refs, outs = refs[:n_out], refs[-n_out:]
        low = l_ref[0]
        for c_ref, out in zip(c_refs, outs):
            out[0] = nn(c_ref[...], low).astype(BF16)

    def corner_spec(d):
        return pl.BlockSpec((rows, CHI), lambda k, me: (me[0] ^ d, 0))

    return pl.pallas_call(
        kernel,
        grid_spec=pltpu.PrefetchScalarGridSpec(
            num_scalar_prefetch=1,
            grid=(count,),
            in_specs=[pl.BlockSpec((1, CHI, rows), lambda k, me: (first + k, 0, 0))]
            + [corner_spec(d) for d in ds] + [ANYWHERE] * len(after),
            out_specs=[pl.BlockSpec((1, rows, rows), lambda k, me: (k, 0, 0))] * n_out,
        ),
        out_shape=[jax.ShapeDtypeStruct((count, rows, rows), BF16)] * n_out,
        compiler_params=params(),
        cost_estimate=cost(count),
        name="absorbed",
    )(me, lower, *[corner_t] * n_out, *after)


def half_chunk(me, blocks, lower, corner, held, first, count, after):
    rows = lower.shape[2]
    n = CHI // rows
    step = 2
    n_held = 0 if held is None else 2

    def kernel(me_ref, l_ref, *refs):
        f_refs, c_refs = refs[:n], refs[n:2 * n]
        half_ref, corner_ref, pair_ref = refs[-3:]

        @pl.when(pl.program_id(0) == 0)
        def _():
            if n_held:
                corner_ref[...] = refs[-5][...]
                pair_ref[...] = refs[-4][...]
            else:
                corner_ref[...] = jnp.zeros_like(corner_ref)
                pair_ref[...] = jnp.zeros_like(pair_ref)

        for j in range(step):
            total = nn(c_refs[0][...], f_refs[0][j])
            for d in range(1, n):
                total += nn(c_refs[d][...], f_refs[d][j])
            half_ref[j] = total.astype(BF16)
            part = total * l_ref[j].astype(F32)
            pair_ref[...] += jnp.sum(part.reshape(CHI // 8, 8, rows), axis=0)
        low = jnp.concatenate([l_ref[j] for j in range(step)], axis=1)
        for d in range(n):
            full = jnp.concatenate([f_refs[d][j] for j in range(step)], axis=1)
            place = pl.ds(pl.multiple_of((me_ref[0] ^ d) * rows, rows), rows)
            corner_ref[:, place] += nt(low, full)

    def corner_spec(d):
        return pl.BlockSpec((CHI, rows), lambda k, me: (0, me[0] ^ d))

    def block_spec(offset):
        return pl.BlockSpec((step, rows, rows), lambda k, me: (offset // step + k, 0, 0))

    corner_sum = pl.BlockSpec((CHI, CHI), lambda k, me: (0, 0))
    pair_sum = pl.BlockSpec((8, rows), lambda k, me: (0, 0))
    operands = [me, lower, *[x for x, _ in blocks], *[corner] * n, *after]
    operands += held if n_held else []
    return pl.pallas_call(
        kernel,
        grid_spec=pltpu.PrefetchScalarGridSpec(
            num_scalar_prefetch=1,
            grid=(count // step,),
            in_specs=[pl.BlockSpec((step, CHI, rows), lambda k, me: (first // step + k, 0, 0))]
            + [block_spec(offset) for _, offset in blocks]
            + [corner_spec(d) for d in range(n)] + [ANYWHERE] * len(after)
            + [corner_sum, pair_sum][:n_held],
            out_specs=[
                pl.BlockSpec((step, CHI, rows), lambda k, me: (k, 0, 0)),
                corner_sum,
                pair_sum,
            ],
        ),
        out_shape=[
            jax.ShapeDtypeStruct((count, CHI, rows), BF16),
            jax.ShapeDtypeStruct((CHI, CHI), F32),
            jax.ShapeDtypeStruct((8, rows), F32),
        ],
        compiler_params=params(),
        cost_estimate=cost(2 * count),
        name="grad_half",
    )(*operands)


def edge_chunk(me, blocks, grad_new, held, first, count, after):
    rows = blocks[0][0].shape[1]
    n = CHI // rows
    has_held = held is not None

    def kernel(me_ref, *refs):
        a_refs, g_refs, out = refs[:n], refs[n:2 * n], refs[-1]
        total = nn(a_refs[0][0], g_refs[0][...])
        for d in range(1, n):
            total += nn(a_refs[d][0], g_refs[d][...])
        out[...] = total.astype(BF16)

    def grad_spec(d):
        return pl.BlockSpec((rows, CHI), lambda k, me: (me[0] ^ d, 0))

    def block_spec(offset):
        return pl.BlockSpec((1, rows, rows), lambda k, me: (offset + k, 0, 0))

    operands = [me, *[x for x, _ in blocks], *[grad_new] * n, *after]
    operands += [held] if has_held else []
    return pl.pallas_call(
        kernel,
        grid_spec=pltpu.PrefetchScalarGridSpec(
            num_scalar_prefetch=1,
            grid=(count,),
            in_specs=[block_spec(offset) for _, offset in blocks]
            + [grad_spec(d) for d in range(n)] + [ANYWHERE] * (len(after) + has_held),
            out_specs=pl.BlockSpec((rows, CHI), lambda k, me: (0, first + k)),
        ),
        out_shape=jax.ShapeDtypeStruct((rows, HALF * CHI), BF16),
        input_output_aliases={len(operands) - 1: 0} if has_held else {},
        compiler_params=params(),
        cost_estimate=cost(count),
        name="grad_edge",
    )(*operands)


def exchanged(blocks):
    far_first = {d: swapped(blocks[d], d) for d in reversed(range(1, len(blocks)))}
    return [blocks[0]] + [far_first[d] for d in range(1, len(blocks))]


def same_charge(rows_ref, columns_ref, x):
    return jnp.where(rows_ref[...] == columns_ref[...], x, 0.0)


def masked_corner(corner, row_charge, column_charge, after):
    rows = CHI // ENV

    def kernel(x_ref, r_ref, c_ref, *refs):
        masked = same_charge(r_ref, c_ref, x_ref[...].astype(F32)).astype(BF16)
        refs[-2][...] = masked
        refs[-1][...] = masked.T

    return pl.pallas_call(
        kernel,
        grid=(ENV,),
        in_specs=[
            pl.BlockSpec((rows, CHI), lambda j: (j, 0)),
            pl.BlockSpec((rows, 1), lambda j: (j, 0)),
            pl.BlockSpec((1, CHI), lambda j: (0, 0)),
        ] + [ANYWHERE] * len(after),
        out_specs=[
            pl.BlockSpec((rows, CHI), lambda j: (j, 0)),
            pl.BlockSpec((CHI, rows), lambda j: (0, j)),
        ],
        out_shape=[jax.ShapeDtypeStruct((CHI, CHI), BF16)] * 2,
        compiler_params=params(),
        cost_estimate=cost(1),
        name="near_corner",
    )(corner, row_charge, column_charge, *after)


def corner_halves(me, total, after):
    rows = CHI // ENV

    def kernel(me_ref, total_ref, *refs):
        refs[-1][0] = total_ref[...].astype(BF16)

    return pl.pallas_call(
        kernel,
        grid_spec=pltpu.PrefetchScalarGridSpec(
            num_scalar_prefetch=1,
            grid=(2,),
            in_specs=[pl.BlockSpec((rows, CHI), lambda h, me: (2 * h + 1 - me[0] % 2, 0))]
            + [ANYWHERE] * len(after),
            out_specs=pl.BlockSpec((1, rows, CHI), lambda h, me: (h, 0, 0)),
        ),
        out_shape=jax.ShapeDtypeStruct((2, rows, CHI), BF16),
        compiler_params=params(),
        cost_estimate=cost(1),
        name="corner_halves",
    )(me, total, *after)


def corner_quarter(me, total, halves, after):
    rows = CHI // ENV

    def kernel(me_ref, total_ref, half_ref, *refs):
        refs[-1][...] = (total_ref[...] + half_ref[0].astype(F32)).astype(BF16)

    return pl.pallas_call(
        kernel,
        grid_spec=pltpu.PrefetchScalarGridSpec(
            num_scalar_prefetch=1,
            grid=(1,),
            in_specs=[
                pl.BlockSpec((rows, CHI), lambda q, me: (me[0] ^ 2, 0)),
                pl.BlockSpec((1, rows, CHI), lambda q, me: ((me[0] ^ 2) // 2, 0, 0)),
            ] + [ANYWHERE] * len(after),
            out_specs=pl.BlockSpec((rows, CHI), lambda q, me: (0, 0)),
        ),
        out_shape=jax.ShapeDtypeStruct((rows, CHI), BF16),
        compiler_params=params(),
        cost_estimate=cost(1),
        name="corner_quarter",
    )(me, total, halves, *after)


def corner_rows(me, total, halves, quarter, charges, after):
    rows = CHI // ENV

    def kernel(me_ref, total_ref, half_ref, quarter_ref, r_ref, c_ref, *refs):
        whole = total_ref[...] + half_ref[0].astype(F32) + quarter_ref[...].astype(F32)
        refs[-1][...] = same_charge(r_ref, c_ref, whole).astype(BF16)

    return pl.pallas_call(
        kernel,
        grid_spec=pltpu.PrefetchScalarGridSpec(
            num_scalar_prefetch=1,
            grid=(1,),
            in_specs=[
                pl.BlockSpec((rows, CHI), lambda q, me: (me[0], 0)),
                pl.BlockSpec((1, rows, CHI), lambda q, me: (me[0] // 2, 0, 0)),
                pl.BlockSpec((rows, CHI), lambda q, me: (0, 0)),
                pl.BlockSpec((rows, 1), lambda q, me: (me[0], 0)),
                pl.BlockSpec((1, CHI), lambda q, me: (0, 0)),
            ] + [ANYWHERE] * len(after),
            out_specs=pl.BlockSpec((rows, CHI), lambda q, me: (0, 0)),
        ),
        out_shape=jax.ShapeDtypeStruct((rows, CHI), BF16),
        compiler_params=params(),
        cost_estimate=cost(1),
        name="grad_corner",
    )(me, total, halves, quarter, *charges, *after)


def charge_masks(parity):
    charges = jnp.repeat(parity, BLK, axis=1)
    corner_mask = charges[0][:, None] == charges[1][None, :]
    out_mask = charges[2][:, None] == charges[3][None, :]
    return corner_mask, out_mask


def spans(counts):
    return [(sum(counts[:j]), count) for j, count in enumerate(counts)]


def chunked_shards(corner, top_edge, half_system, values, cotangent, parity):
    rows = CHI // ENV
    me = lax.axis_index("env").astype(jnp.int32)
    me_arr = me.reshape(1)
    near_corner = row_major(corner_moved(row_major(corner[0, 0]), 1))
    above = jnp.repeat(passed_along(parity[0, 0], "row", 1), BLK, axis=1)
    row_charge, column_charge = above[0][:, None], above[1][None, :]
    _, out_mask = charge_masks(parity[0, 0])
    grad_new = jnp.where(
        out_mask, values[0, 0][:, None] ** (-0.5) * cotangent[0, 0].astype(F32), 0.0
    ).astype(BF16)
    top, half = top_edge[0, 0], half_system[0, 0]
    full_spans, edge_spans = spans(FULL_CHUNKS), spans(EDGE_CHUNKS)

    full_far, full_near, edge_far, edge_near, half_parts = {}, [], {}, [], []
    totals = halves = quarter = grad_corner = grad_edge = grad_half = None
    last = []
    for step in ORDER.split():
        what, j = step[0], int(step[1:] or 0)
        if what == "F":
            blocks = full_chunk(me_arr, top, grad_new, (3, 2), *full_spans[j], last)
            last = [blocks[0]]
            if j in HELD_BACK:
                blocks = held_back(blocks, full_far[HELD_BACK[j]])
                last = [blocks[0]]
            full_far[j] = [swapped(blocks[0], 3, 1), swapped(blocks[1], 2, 1)]
        elif what == "f":
            blocks = full_chunk(me_arr, top, grad_new, (0, 1), 0, HALF, last)
            last = [blocks[0]]
            full_near = [swapped(blocks[0], 0, 1), swapped(blocks[1], 1, 1)]
        elif what == "C":
            near_corner, corner_t = masked_corner(near_corner, row_charge, column_charge, last)
            last = [corner_t]
        elif what == "T":
            lower = k_major(half, last)
            last = [lower]
        elif what == "A":
            blocks = absorbed_chunk(me_arr, lower, corner_t, (3, 2), *edge_spans[j], last)
            last = [blocks[0]]
            edge_far[j] = [swapped(blocks[0], 3, -1), swapped(blocks[1], 2, -1)]
        elif what == "a":
            blocks = absorbed_chunk(me_arr, lower, corner_t, (0, 1), 0, HALF, last)
            last = [blocks[0]]
            edge_near = [swapped(blocks[0], 0, -1), swapped(blocks[1], 1, -1)]
        elif what == "H":
            first, count = full_spans[j]
            blocks = [(x, first) for x in full_near] + [(x, 0) for x in reversed(full_far[j])]
            part, *totals = half_chunk(
                me_arr, blocks, lower, near_corner, totals, first, count, last
            )
            last = [totals[1]]
            half_parts.append(part)
        elif what == "M":
            grad_half = k_minor(half_parts, last)
            last = [grad_half]
        elif what == "R" and j == 1:
            halves = corner_halves(me_arr, totals[0], last)
            last = [halves]
            halves = swapped(halves, 1)
        elif what == "R" and j == 2:
            quarter = corner_quarter(me_arr, totals[0], halves, last)
            last = [quarter]
            quarter = swapped(quarter, 2)
        elif what == "R" and j == 3:
            charged = (row_charge, column_charge)
            grad_corner = corner_rows(me_arr, totals[0], halves, quarter, charged, last)
            last = [grad_corner]
            grad_corner = corner_moved(grad_corner, -1)
        elif what == "R":
            last = last + [grad_corner]
        elif what == "W":
            last = last + full_far[j]
        elif what == "w":
            last = last + full_near
        elif what == "E":
            first, count = edge_spans[j]
            blocks = [(x, first) for x in edge_near] + [(x, 0) for x in reversed(edge_far[j])]
            grad_edge = edge_chunk(
                me_arr, blocks, grad_new, grad_edge, first, count,
                [x for x in last if x is not grad_edge],
            )
            last = [grad_edge]
    own_values = lax.dynamic_slice_in_dim(values[0, 0], me * rows, rows, 0)
    pair_sums = passed_along(jnp.sum(totals[1], axis=0), "row", -1)
    grad_values = -0.5 * pair_sums / own_values

    return (
        grad_corner[None, None],
        grad_edge[None, None],
        grad_half[None, None],
        grad_values[None, None],
    )


def whole_shards(corner, top_edge, half_system, values, cotangent, parity):
    rows = top_edge.shape[2]
    row_start = lax.axis_index("env") * rows
    corner_mask, out_mask = charge_masks(parity[0, 0])
    near_corner = passed_along(corner[0, 0], "col", 1)
    near_corner = jnp.where(corner_mask, near_corner, jnp.zeros_like(near_corner))
    lower_half = passed_along(half_system[0, 0], "row", -1).reshape(rows, CHI, HALF)
    absorbed = jnp.einsum("ab,iak->ibk", near_corner, lower_half, preferred_element_type=F32)
    absorbed = absorbed.astype(BF16).reshape(rows, CHI * HALF)
    gathered = lax.all_to_all(absorbed, "env", split_axis=1, concat_axis=0, tiled=True)
    edge_mat = top_edge[0, 0].reshape(rows * HALF, CHI)
    grad_new = jnp.where(
        out_mask, values[0, 0][:, None] ** (-0.5) * cotangent[0, 0].astype(F32), 0.0
    ).astype(BF16)
    grad_edge = jnp.einsum("ij,ie->je", gathered, grad_new, preferred_element_type=F32)
    grad_edge = grad_edge.astype(BF16).reshape(rows, HALF * CHI)
    grad_full = jnp.einsum("ie,je->ij", grad_new, edge_mat, preferred_element_type=F32)
    totals = lax.psum(jnp.sum(gathered * grad_full, axis=1), "env")
    pair_sums = lax.dynamic_slice_in_dim(totals, row_start, rows, 0)
    own_values = lax.dynamic_slice_in_dim(values[0, 0], row_start, rows, 0)
    grad_values = -0.5 * pair_sums / own_values
    grad_back = lax.all_to_all(
        grad_full.astype(BF16), "env", split_axis=0, concat_axis=1, tiled=True
    ).reshape(rows, CHI, HALF)
    grad_half = jnp.einsum("ab,ibk->iak", near_corner, grad_back, preferred_element_type=F32)
    grad_half = grad_half.astype(BF16).reshape(rows, CHI * HALF)
    summed = jnp.einsum("iak,ibk->ab", lower_half, grad_back, preferred_element_type=F32)
    summed = lax.psum_scatter(summed, "env", scatter_dimension=0, tiled=True)
    own_mask = lax.dynamic_slice_in_dim(corner_mask, row_start, rows, 0)
    grad_corner = jnp.where(own_mask, summed, 0.0).astype(BF16)
    grad_corner = passed_along(grad_corner, "col", -1)
    grad_half = passed_along(grad_half, "row", 1)
    return (
        grad_corner[None, None],
        grad_edge[None, None],
        grad_half[None, None],
        grad_values[None, None],
    )


def solution(mesh):
    chunked = mesh.shape["env"] == ENV
    return jax.shard_map(
        chunked_shards if chunked else whole_shards,
        mesh=mesh,
        in_specs=(
            P("row", "col", None, None),
            P("row", "col", "env", None),
            P("row", "col", "env", None),
            P("row", "col", None),
            P("row", "col", None, None),
            P("row", "col", None, None),
        ),
        out_specs=(
            P("row", "col", "env", None),
            P("row", "col", "env", None),
            P("row", "col", "env", None),
            P("row", "col", "env"),
        ),
        check_vma=False,
    )
```

```python
import functools

import jax
import jax.numpy as jnp
from jax import lax
from jax.experimental import pallas as pl
from jax.experimental.layout import Layout, with_layout_constraint
from jax.experimental.pallas import tpu as pltpu
from jax.sharding import PartitionSpec as P

CHI = 1024
HALF = 32
BLK = 128

FULL_CHUNKS = (4, 28)
EDGE_CHUNKS = (9, 9, 6, 4, 3, 1)
ENV = 4

MIB = 1 << 20
VMEM_MIB = 56
COST_BITS = 20
CORNER_FIRST = 1
HELD_BACK = {1: (2, 3)}
ORDER = "F0 F1 C T A0 a A1 H0 H1 R1 A2 E0 A3 R2 M E1 A4 R3 E2 A5 E3 R4 E4 E5"
F32 = jnp.float32
BF16 = jnp.bfloat16


def passed_along(x, axis, by):
    size = lax.axis_size(axis)
    return lax.ppermute(x, axis, [(i, (i + by) % size) for i in range(size)])


def swapped(x, d, rows_on=0):
    n_row, n_env = lax.axis_size("row"), lax.axis_size("env")
    if not rows_on:
        return lax.ppermute(x, "env", [(i, i ^ d) for i in range(n_env)])
    pairs = [
        (r * n_env + i, (r + rows_on) % n_row * n_env + (i ^ d))
        for r in range(n_row) for i in range(n_env)
    ]
    return lax.ppermute(x, ("row", "env"), pairs)


def corner_moved(x, by):
    n_row, n_col = lax.axis_size("row"), lax.axis_size("col")
    pairs = [
        (r * n_col + c, (r + by) % n_row * n_col + (c + by) % n_col)
        for r in range(n_row) for c in range(n_col)
    ]
    return lax.ppermute(x, ("row", "col"), pairs)


def nn(a, b):
    return jnp.dot(a, b, preferred_element_type=F32)


def nt(a, b):
    return lax.dot_general(a, b, (((1,), (1,)), ((), ())), preferred_element_type=F32)


ANYWHERE = pl.BlockSpec(memory_space=pl.ANY)


def params(dims=1):
    return pltpu.CompilerParams(
        vmem_limit_bytes=VMEM_MIB * MIB, dimension_semantics=("arbitrary",) * dims
    )


def cost(count):
    return pl.CostEstimate(
        flops=count << COST_BITS, bytes_accessed=count << (COST_BITS - 8), transcendentals=0
    )


def row_major(x):
    return with_layout_constraint(x, Layout(tuple(range(x.ndim))))


def full_chunk(me, top_edge, grad_new, ds, first, count, after):
    rows = top_edge.shape[0]
    n_out = len(ds)

    def kernel(me_ref, t_ref, *refs):
        g_refs, outs = refs[:n_out], refs[-n_out:]
        t = t_ref[...]
        for g_ref, out in zip(g_refs, outs):
            out[0] = nt(t, g_ref[...]).astype(BF16)

    def grad_spec(d):
        return pl.BlockSpec((rows, CHI), lambda k, me: (me[0] ^ d, 0))

    return pl.pallas_call(
        kernel,
        grid_spec=pltpu.PrefetchScalarGridSpec(
            num_scalar_prefetch=1,
            grid=(count,),
            in_specs=[pl.BlockSpec((rows, CHI), lambda k, me: (0, first + k))]
            + [grad_spec(d) for d in ds] + [ANYWHERE] * len(after),
            out_specs=[pl.BlockSpec((1, rows, rows), lambda k, me: (k, 0, 0))] * n_out,
        ),
        out_shape=[jax.ShapeDtypeStruct((count, rows, rows), BF16)] * n_out,
        compiler_params=params(),
        cost_estimate=cost(count),
        name="grad_full",
    )(me, top_edge, *[grad_new] * n_out, *after)


GROUP = 64


def k_major(x, after):
    rows = x.shape[0]

    def kernel(x_ref, *refs):
        turned = x_ref[...].T.reshape(GROUP, HALF, rows)
        refs[-1][...] = jnp.transpose(turned, (1, 0, 2))

    return pl.pallas_call(
        kernel,
        grid=(CHI // GROUP,),
        in_specs=[pl.BlockSpec((rows, GROUP * HALF), lambda j: (0, j))] + [ANYWHERE] * len(after),
        out_specs=pl.BlockSpec((HALF, GROUP, rows), lambda j: (0, j, 0)),
        out_shape=jax.ShapeDtypeStruct((HALF, CHI, rows), BF16),
        compiler_params=params(),
        cost_estimate=cost(1),
        name="k_major",
    )(x, *after)


def k_minor(parts, after):
    rows = parts[0].shape[2]
    n_parts = len(parts)

    def kernel(*refs):
        whole = jnp.concatenate([ref[...] for ref in refs[:n_parts]], axis=0)
        refs[-1][...] = jnp.transpose(whole, (1, 0, 2)).reshape(GROUP * HALF, rows).T

    return pl.pallas_call(
        kernel,
        grid=(CHI // GROUP,),
        in_specs=[pl.BlockSpec((x.shape[0], GROUP, rows), lambda j: (0, j, 0)) for x in parts]
        + [ANYWHERE] * len(after),
        out_specs=pl.BlockSpec((rows, GROUP * HALF), lambda j: (0, j)),
        out_shape=jax.ShapeDtypeStruct((rows, CHI * HALF), BF16),
        compiler_params=params(),
        cost_estimate=cost(1),
        name="k_minor",
    )(*parts, *after)


def held_back(arrays, after):
    n_arrays = len(arrays)
    return pl.pallas_call(
        lambda *refs: None,
        in_specs=[ANYWHERE] * (n_arrays + len(after)),
        out_specs=[ANYWHERE] * n_arrays,
        out_shape=[jax.ShapeDtypeStruct(x.shape, x.dtype) for x in arrays],
        input_output_aliases={j: j for j in range(n_arrays)},
        compiler_params=pltpu.CompilerParams(vmem_limit_bytes=VMEM_MIB * MIB),
        cost_estimate=cost(1),
        name="held_back",
    )(*arrays, *after)


def absorbed_chunk(me, lower, corner_t, ds, first, count, after):
    rows = lower.shape[2]
    n_out = len(ds)

    def kernel(me_ref, l_ref, *refs):
        c_refs, outs = refs[:n_out], refs[-n_out:]
        low = l_ref[0]
        for c_ref, out in zip(c_refs, outs):
            out[0] = nn(c_ref[...], low).astype(BF16)

    def corner_spec(d):
        return pl.BlockSpec((rows, CHI), lambda k, me: (me[0] ^ d, 0))

    return pl.pallas_call(
        kernel,
        grid_spec=pltpu.PrefetchScalarGridSpec(
            num_scalar_prefetch=1,
            grid=(count,),
            in_specs=[pl.BlockSpec((1, CHI, rows), lambda k, me: (first + k, 0, 0))]
            + [corner_spec(d) for d in ds] + [ANYWHERE] * len(after),
            out_specs=[pl.BlockSpec((1, rows, rows), lambda k, me: (k, 0, 0))] * n_out,
        ),
        out_shape=[jax.ShapeDtypeStruct((count, rows, rows), BF16)] * n_out,
        compiler_params=params(),
        cost_estimate=cost(count),
        name="absorbed",
    )(me, lower, *[corner_t] * n_out, *after)


def half_chunk(me, blocks, lower, corner, held, first, count, after):
    rows = lower.shape[2]
    n = CHI // rows
    step = 2
    n_held = 0 if held is None else 2

    def kernel(me_ref, l_ref, *refs):
        f_refs, c_refs = refs[:n], refs[n:2 * n]
        half_ref, corner_ref, pair_ref = refs[-3:]

        @pl.when(pl.program_id(0) == 0)
        def _():
            if n_held:
                corner_ref[...] = refs[-5][...]
                pair_ref[...] = refs[-4][...]
            else:
                corner_ref[...] = jnp.zeros_like(corner_ref)
                pair_ref[...] = jnp.zeros_like(pair_ref)

        for j in range(step):
            total = nn(c_refs[0][...], f_refs[0][j])
            for d in range(1, n):
                total += nn(c_refs[d][...], f_refs[d][j])
            half_ref[j] = total.astype(BF16)
            part = total * l_ref[j].astype(F32)
            pair_ref[...] += jnp.sum(part.reshape(CHI // 8, 8, rows), axis=0)
        low = jnp.concatenate([l_ref[j] for j in range(step)], axis=1)
        for d in range(n):
            full = jnp.concatenate([f_refs[d][j] for j in range(step)], axis=1)
            place = pl.ds(pl.multiple_of((me_ref[0] ^ d) * rows, rows), rows)
            corner_ref[:, place] += nt(low, full)

    def corner_spec(d):
        return pl.BlockSpec((CHI, rows), lambda k, me: (0, me[0] ^ d))

    def block_spec(offset):
        return pl.BlockSpec((step, rows, rows), lambda k, me: (offset // step + k, 0, 0))

    corner_sum = pl.BlockSpec((CHI, CHI), lambda k, me: (0, 0))
    pair_sum = pl.BlockSpec((8, rows), lambda k, me: (0, 0))
    operands = [me, lower, *[x for x, _ in blocks], *[corner] * n, *after]
    operands += held if n_held else []
    return pl.pallas_call(
        kernel,
        grid_spec=pltpu.PrefetchScalarGridSpec(
            num_scalar_prefetch=1,
            grid=(count // step,),
            in_specs=[pl.BlockSpec((step, CHI, rows), lambda k, me: (first // step + k, 0, 0))]
            + [block_spec(offset) for _, offset in blocks]
            + [corner_spec(d) for d in range(n)] + [ANYWHERE] * len(after)
            + [corner_sum, pair_sum][:n_held],
            out_specs=[
                pl.BlockSpec((step, CHI, rows), lambda k, me: (k, 0, 0)),
                corner_sum,
                pair_sum,
            ],
        ),
        out_shape=[
            jax.ShapeDtypeStruct((count, CHI, rows), BF16),
            jax.ShapeDtypeStruct((CHI, CHI), F32),
            jax.ShapeDtypeStruct((8, rows), F32),
        ],
        compiler_params=params(),
        cost_estimate=cost(2 * count),
        name="grad_half",
    )(*operands)


def edge_chunk(me, blocks, grad_new, held, first, count, after):
    rows = blocks[0][0].shape[1]
    n = CHI // rows
    has_held = held is not None

    def kernel(me_ref, *refs):
        a_refs, g_refs, out = refs[:n], refs[n:2 * n], refs[-1]
        total = nn(a_refs[0][0], g_refs[0][...])
        for d in range(1, n):
            total += nn(a_refs[d][0], g_refs[d][...])
        out[...] = total.astype(BF16)

    def grad_spec(d):
        return pl.BlockSpec((rows, CHI), lambda k, me: (me[0] ^ d, 0))

    def block_spec(offset):
        return pl.BlockSpec((1, rows, rows), lambda k, me: (offset + k, 0, 0))

    operands = [me, *[x for x, _ in blocks], *[grad_new] * n, *after]
    operands += [held] if has_held else []
    return pl.pallas_call(
        kernel,
        grid_spec=pltpu.PrefetchScalarGridSpec(
            num_scalar_prefetch=1,
            grid=(count,),
            in_specs=[block_spec(offset) for _, offset in blocks]
            + [grad_spec(d) for d in range(n)] + [ANYWHERE] * (len(after) + has_held),
            out_specs=pl.BlockSpec((rows, CHI), lambda k, me: (0, first + k)),
        ),
        out_shape=jax.ShapeDtypeStruct((rows, HALF * CHI), BF16),
        input_output_aliases={len(operands) - 1: 0} if has_held else {},
        compiler_params=params(),
        cost_estimate=cost(count),
        name="grad_edge",
    )(*operands)


def exchanged(blocks):
    far_first = {d: swapped(blocks[d], d) for d in reversed(range(1, len(blocks)))}
    return [blocks[0]] + [far_first[d] for d in range(1, len(blocks))]


def same_charge(rows_ref, columns_ref, x):
    return jnp.where(rows_ref[...] == columns_ref[...], x, 0.0)


def masked_corner(corner, row_charge, column_charge, after):
    rows = CHI // ENV

    def kernel(x_ref, r_ref, c_ref, *refs):
        masked = same_charge(r_ref, c_ref, x_ref[...].astype(F32)).astype(BF16)
        refs[-2][...] = masked
        refs[-1][...] = masked.T

    return pl.pallas_call(
        kernel,
        grid=(ENV,),
        in_specs=[
            pl.BlockSpec((rows, CHI), lambda j: (j, 0)),
            pl.BlockSpec((rows, 1), lambda j: (j, 0)),
            pl.BlockSpec((1, CHI), lambda j: (0, 0)),
        ] + [ANYWHERE] * len(after),
        out_specs=[
            pl.BlockSpec((rows, CHI), lambda j: (j, 0)),
            pl.BlockSpec((CHI, rows), lambda j: (0, j)),
        ],
        out_shape=[jax.ShapeDtypeStruct((CHI, CHI), BF16)] * 2,
        compiler_params=params(),
        cost_estimate=cost(1),
        name="near_corner",
    )(corner, row_charge, column_charge, *after)


def corner_halves(me, total, after):
    rows = CHI // ENV

    def kernel(me_ref, total_ref, *refs):
        refs[-1][0] = total_ref[...].astype(BF16)

    return pl.pallas_call(
        kernel,
        grid_spec=pltpu.PrefetchScalarGridSpec(
            num_scalar_prefetch=1,
            grid=(2,),
            in_specs=[pl.BlockSpec((rows, CHI), lambda h, me: (2 * h + 1 - me[0] % 2, 0))]
            + [ANYWHERE] * len(after),
            out_specs=pl.BlockSpec((1, rows, CHI), lambda h, me: (h, 0, 0)),
        ),
        out_shape=jax.ShapeDtypeStruct((2, rows, CHI), BF16),
        compiler_params=params(),
        cost_estimate=cost(1),
        name="corner_halves",
    )(me, total, *after)


def corner_quarter(me, total, halves, after):
    rows = CHI // ENV

    def kernel(me_ref, total_ref, half_ref, *refs):
        refs[-1][...] = (total_ref[...] + half_ref[0].astype(F32)).astype(BF16)

    return pl.pallas_call(
        kernel,
        grid_spec=pltpu.PrefetchScalarGridSpec(
            num_scalar_prefetch=1,
            grid=(1,),
            in_specs=[
                pl.BlockSpec((rows, CHI), lambda q, me: (me[0] ^ 2, 0)),
                pl.BlockSpec((1, rows, CHI), lambda q, me: ((me[0] ^ 2) // 2, 0, 0)),
            ] + [ANYWHERE] * len(after),
            out_specs=pl.BlockSpec((rows, CHI), lambda q, me: (0, 0)),
        ),
        out_shape=jax.ShapeDtypeStruct((rows, CHI), BF16),
        compiler_params=params(),
        cost_estimate=cost(1),
        name="corner_quarter",
    )(me, total, halves, *after)


def corner_rows(me, total, halves, quarter, charges, after):
    rows = CHI // ENV

    def kernel(me_ref, total_ref, half_ref, quarter_ref, r_ref, c_ref, *refs):
        whole = total_ref[...] + half_ref[0].astype(F32) + quarter_ref[...].astype(F32)
        refs[-1][...] = same_charge(r_ref, c_ref, whole).astype(BF16)

    return pl.pallas_call(
        kernel,
        grid_spec=pltpu.PrefetchScalarGridSpec(
            num_scalar_prefetch=1,
            grid=(1,),
            in_specs=[
                pl.BlockSpec((rows, CHI), lambda q, me: (me[0], 0)),
                pl.BlockSpec((1, rows, CHI), lambda q, me: (me[0] // 2, 0, 0)),
                pl.BlockSpec((rows, CHI), lambda q, me: (0, 0)),
                pl.BlockSpec((rows, 1), lambda q, me: (me[0], 0)),
                pl.BlockSpec((1, CHI), lambda q, me: (0, 0)),
            ] + [ANYWHERE] * len(after),
            out_specs=pl.BlockSpec((rows, CHI), lambda q, me: (0, 0)),
        ),
        out_shape=jax.ShapeDtypeStruct((rows, CHI), BF16),
        compiler_params=params(),
        cost_estimate=cost(1),
        name="grad_corner",
    )(me, total, halves, quarter, *charges, *after)


def charge_masks(parity):
    charges = jnp.repeat(parity, BLK, axis=1)
    corner_mask = charges[0][:, None] == charges[1][None, :]
    out_mask = charges[2][:, None] == charges[3][None, :]
    return corner_mask, out_mask


def spans(counts):
    return [(sum(counts[:j]), count) for j, count in enumerate(counts)]


def chunked_shards(corner, top_edge, half_system, values, cotangent, parity):
    rows = CHI // ENV
    me = lax.axis_index("env").astype(jnp.int32)
    me_arr = me.reshape(1)
    near_corner = row_major(corner_moved(row_major(corner[0, 0]), 1))
    above = jnp.repeat(passed_along(parity[0, 0], "row", 1), BLK, axis=1)
    row_charge, column_charge = above[0][:, None], above[1][None, :]
    _, out_mask = charge_masks(parity[0, 0])
    grad_new = jnp.where(
        out_mask, values[0, 0][:, None] ** (-0.5) * cotangent[0, 0].astype(F32), 0.0
    ).astype(BF16)
    top, half = top_edge[0, 0], half_system[0, 0]
    full_spans, edge_spans = spans(FULL_CHUNKS), spans(EDGE_CHUNKS)

    full, edge_far, edge_near, half_parts = {}, {}, [], []
    totals = halves = quarter = grad_corner = grad_edge = grad_half = None
    last = []
    for step in ORDER.split():
        what, j = step[0], int(step[1:] or 0)
        if what == "F":
            blocks = full_chunk(me_arr, top, grad_new, (3, 2, 1, 0), *full_spans[j], last)
            last = [blocks[0]]
            if j in HELD_BACK:
                blocks = held_back(blocks, [full[j - 1][d] for d in HELD_BACK[j]] + [near_corner] * CORNER_FIRST)
                last = [blocks[0]]
            full[j] = [swapped(x, 3 - d, 1) for d, x in enumerate(blocks)][::-1]
        elif what == "C":
            near_corner, corner_t = masked_corner(near_corner, row_charge, column_charge, last)
            last = [corner_t]
        elif what == "T":
            lower = k_major(half, last)
            last = [lower]
        elif what == "A":
            blocks = absorbed_chunk(me_arr, lower, corner_t, (3, 2), *edge_spans[j], last)
            last = [blocks[0]]
            edge_far[j] = [swapped(blocks[0], 3, -1), swapped(blocks[1], 2, -1)]
        elif what == "a":
            blocks = absorbed_chunk(me_arr, lower, corner_t, (0, 1), 0, HALF, last)
            last = [blocks[0]]
            edge_near = [swapped(blocks[0], 0, -1), swapped(blocks[1], 1, -1)]
        elif what == "H":
            first, count = full_spans[j]
            blocks = [(x, 0) for x in full[j]]
            part, *totals = half_chunk(
                me_arr, blocks, lower, near_corner, totals, first, count, last
            )
            last = [totals[1]]
            half_parts.append(part)
        elif what == "M":
            grad_half = k_minor(half_parts, last)
            last = [grad_half]
        elif what == "R" and j == 1:
            halves = corner_halves(me_arr, totals[0], last)
            last = [halves]
            halves = swapped(halves, 1)
        elif what == "R" and j == 2:
            quarter = corner_quarter(me_arr, totals[0], halves, last)
            last = [quarter]
            quarter = swapped(quarter, 2)
        elif what == "R" and j == 3:
            charged = (row_charge, column_charge)
            grad_corner = corner_rows(me_arr, totals[0], halves, quarter, charged, last)
            last = [grad_corner]
            grad_corner = corner_moved(grad_corner, -1)
        elif what == "R":
            last = last + [grad_corner]
        elif what == "W":
            last = last + full[j]
        elif what == "w":
            last = last + full[j][:2]
        elif what == "E":
            first, count = edge_spans[j]
            blocks = [(x, first) for x in edge_near] + [(x, 0) for x in reversed(edge_far[j])]
            grad_edge = edge_chunk(
                me_arr, blocks, grad_new, grad_edge, first, count,
                [x for x in last if x is not grad_edge],
            )
            last = [grad_edge]
    own_values = lax.dynamic_slice_in_dim(values[0, 0], me * rows, rows, 0)
    pair_sums = passed_along(jnp.sum(totals[1], axis=0), "row", -1)
    grad_values = -0.5 * pair_sums / own_values

    return (
        grad_corner[None, None],
        grad_edge[None, None],
        grad_half[None, None],
        grad_values[None, None],
    )


def whole_shards(corner, top_edge, half_system, values, cotangent, parity):
    rows = top_edge.shape[2]
    row_start = lax.axis_index("env") * rows
    corner_mask, out_mask = charge_masks(parity[0, 0])
    near_corner = passed_along(corner[0, 0], "col", 1)
    near_corner = jnp.where(corner_mask, near_corner, jnp.zeros_like(near_corner))
    lower_half = passed_along(half_system[0, 0], "row", -1).reshape(rows, CHI, HALF)
    absorbed = jnp.einsum("ab,iak->ibk", near_corner, lower_half, preferred_element_type=F32)
    absorbed = absorbed.astype(BF16).reshape(rows, CHI * HALF)
    gathered = lax.all_to_all(absorbed, "env", split_axis=1, concat_axis=0, tiled=True)
    edge_mat = top_edge[0, 0].reshape(rows * HALF, CHI)
    grad_new = jnp.where(
        out_mask, values[0, 0][:, None] ** (-0.5) * cotangent[0, 0].astype(F32), 0.0
    ).astype(BF16)
    grad_edge = jnp.einsum("ij,ie->je", gathered, grad_new, preferred_element_type=F32)
    grad_edge = grad_edge.astype(BF16).reshape(rows, HALF * CHI)
    grad_full = jnp.einsum("ie,je->ij", grad_new, edge_mat, preferred_element_type=F32)
    totals = lax.psum(jnp.sum(gathered * grad_full, axis=1), "env")
    pair_sums = lax.dynamic_slice_in_dim(totals, row_start, rows, 0)
    own_values = lax.dynamic_slice_in_dim(values[0, 0], row_start, rows, 0)
    grad_values = -0.5 * pair_sums / own_values
    grad_back = lax.all_to_all(
        grad_full.astype(BF16), "env", split_axis=0, concat_axis=1, tiled=True
    ).reshape(rows, CHI, HALF)
    grad_half = jnp.einsum("ab,ibk->iak", near_corner, grad_back, preferred_element_type=F32)
    grad_half = grad_half.astype(BF16).reshape(rows, CHI * HALF)
    summed = jnp.einsum("iak,ibk->ab", lower_half, grad_back, preferred_element_type=F32)
    summed = lax.psum_scatter(summed, "env", scatter_dimension=0, tiled=True)
    own_mask = lax.dynamic_slice_in_dim(corner_mask, row_start, rows, 0)
    grad_corner = jnp.where(own_mask, summed, 0.0).astype(BF16)
    grad_corner = passed_along(grad_corner, "col", -1)
    grad_half = passed_along(grad_half, "row", 1)
    return (
        grad_corner[None, None],
        grad_edge[None, None],
        grad_half[None, None],
        grad_values[None, None],
    )


def solution(mesh):
    chunked = mesh.shape["env"] == ENV
    return jax.shard_map(
        chunked_shards if chunked else whole_shards,
        mesh=mesh,
        in_specs=(
            P("row", "col", None, None),
            P("row", "col", "env", None),
            P("row", "col", "env", None),
            P("row", "col", None),
            P("row", "col", None, None),
            P("row", "col", None, None),
        ),
        out_specs=(
            P("row", "col", "env", None),
            P("row", "col", "env", None),
            P("row", "col", "env", None),
            P("row", "col", "env"),
        ),
        check_vma=False,
    )
```

```python
import functools

import jax
import jax.numpy as jnp
from jax import lax
from jax.experimental import pallas as pl
from jax.experimental.layout import Layout, with_layout_constraint
from jax.experimental.pallas import tpu as pltpu
from jax.sharding import PartitionSpec as P

CHI = 1024
HALF = 32
BLK = 128

FULL_CHUNKS = (4, 28)
EDGE_CHUNKS = (9, 9, 6, 4, 3, 1)
ENV = 4

MIB = 1 << 20
VMEM_MIB = 56
COST_BITS = 20
CORNER_FIRST = 1
HELD_BACK = {1: (2, 3)}
ORDER = "F0 F1 C T A0 a A1 H0 H1 R1 A2 E0 A3 R2 M E1 A4 R3 E2 A5 E3 R4 E4 E5"
F32 = jnp.float32
BF16 = jnp.bfloat16


def passed_along(x, axis, by):
    size = lax.axis_size(axis)
    return lax.ppermute(x, axis, [(i, (i + by) % size) for i in range(size)])


def swapped(x, d, rows_on=0):
    n_row, n_env = lax.axis_size("row"), lax.axis_size("env")
    if not rows_on:
        return lax.ppermute(x, "env", [(i, i ^ d) for i in range(n_env)])
    pairs = [
        (r * n_env + i, (r + rows_on) % n_row * n_env + (i ^ d))
        for r in range(n_row) for i in range(n_env)
    ]
    return lax.ppermute(x, ("row", "env"), pairs)


def corner_moved(x, by):
    n_row, n_col = lax.axis_size("row"), lax.axis_size("col")
    pairs = [
        (r * n_col + c, (r + by) % n_row * n_col + (c + by) % n_col)
        for r in range(n_row) for c in range(n_col)
    ]
    return lax.ppermute(x, ("row", "col"), pairs)


def nn(a, b):
    return jnp.dot(a, b, preferred_element_type=F32)


def nt(a, b):
    return lax.dot_general(a, b, (((1,), (1,)), ((), ())), preferred_element_type=F32)


ANYWHERE = pl.BlockSpec(memory_space=pl.ANY)


def params(dims=1):
    return pltpu.CompilerParams(
        vmem_limit_bytes=VMEM_MIB * MIB, dimension_semantics=("arbitrary",) * dims
    )


def cost(count):
    return pl.CostEstimate(
        flops=count << COST_BITS, bytes_accessed=count << (COST_BITS - 8), transcendentals=0
    )


def row_major(x):
    return with_layout_constraint(x, Layout(tuple(range(x.ndim))))


def full_chunk(top_edge, grad_blocks, ds, first, count, after):
    rows = top_edge.shape[0]
    n_out = len(ds)
    step = 2 if first % 2 == 0 and count % 2 == 0 else 1

    def kernel(t_ref, *refs):
        g_refs, outs = refs[:n_out], refs[-n_out:]
        t = jnp.concatenate([t_ref[:, j * CHI:(j + 1) * CHI] for j in range(step)], axis=0)
        for g_ref, out in zip(g_refs, outs):
            out[...] = nt(t, g_ref[...]).astype(BF16).reshape(step, rows, rows)

    return pl.pallas_call(
        kernel,
        grid=(count // step,),
        in_specs=[pl.BlockSpec((rows, step * CHI), lambda k: (0, first // step + k))]
        + [pl.BlockSpec((rows, CHI), lambda k: (0, 0))] * n_out + [ANYWHERE] * len(after),
        out_specs=[pl.BlockSpec((step, rows, rows), lambda k: (k, 0, 0))] * n_out,
        out_shape=[jax.ShapeDtypeStruct((count, rows, rows), BF16)] * n_out,
        compiler_params=params(),
        cost_estimate=cost(count),
        name="grad_full",
    )(top_edge, *[grad_blocks[d] for d in ds], *after)


def first_full_chunk(me, parity, top_edge, values, cotangent, ds, count):
    rows = top_edge.shape[0]
    n = CHI // rows
    step = 2 if count % 2 == 0 else 1

    def kernel(me_ref, parity_ref, t_ref, *refs):
        v_refs, cot_refs, g_refs, outs = refs[:n], refs[n:2 * n], refs[2 * n:3 * n], refs[3 * n:]

        @pl.when(pl.program_id(0) == 0)
        def _():
            for d in range(n):
                weight = jnp.broadcast_to(v_refs[d][...], (8, rows)).T[:, :1] ** (-0.5)
                for i in range(rows // BLK):
                    charge = parity_ref[2, (me_ref[0] ^ d) * (rows // BLK) + i]
                    part = slice(i * BLK, (i + 1) * BLK)
                    for e in range(CHI // BLK):
                        across = slice(e * BLK, (e + 1) * BLK)
                        scaled = weight[part] * cot_refs[d][part, across].astype(F32)
                        kept = jnp.where(charge == parity_ref[3, e], scaled, 0.0)
                        g_refs[d][part, across] = kept.astype(BF16)

        t = jnp.concatenate([t_ref[:, j * CHI:(j + 1) * CHI] for j in range(step)], axis=0)
        for d, out in zip(ds, outs):
            out[...] = nt(t, g_refs[d][...]).astype(BF16).reshape(step, rows, rows)

    def value_spec(d):
        return pl.BlockSpec((1, rows), lambda k, me, parity: (0, me[0] ^ d))

    def cotangent_spec(d):
        return pl.BlockSpec((rows, CHI), lambda k, me, parity: (me[0] ^ d, 0))

    made = pl.pallas_call(
        kernel,
        grid_spec=pltpu.PrefetchScalarGridSpec(
            num_scalar_prefetch=2,
            grid=(count // step,),
            in_specs=[pl.BlockSpec((rows, step * CHI), lambda k, me, parity: (0, k))]
            + [value_spec(d) for d in range(n)] + [cotangent_spec(d) for d in range(n)],
            out_specs=[pl.BlockSpec((rows, CHI), lambda k, me, parity: (0, 0))] * n
            + [pl.BlockSpec((step, rows, rows), lambda k, me, parity: (k, 0, 0))] * len(ds),
        ),
        out_shape=[jax.ShapeDtypeStruct((rows, CHI), BF16)] * n
        + [jax.ShapeDtypeStruct((count, rows, rows), BF16)] * len(ds),
        compiler_params=params(),
        cost_estimate=cost(count),
        name="grad_full",
    )(me, parity, top_edge, *[values] * n, *[cotangent] * n)
    return made[:n], made[n:]


GROUP = 64


def k_major(x, after):
    rows = x.shape[0]

    def kernel(x_ref, *refs):
        turned = x_ref[...].T.reshape(GROUP, HALF, rows)
        refs[-1][...] = jnp.transpose(turned, (1, 0, 2))

    return pl.pallas_call(
        kernel,
        grid=(CHI // GROUP,),
        in_specs=[pl.BlockSpec((rows, GROUP * HALF), lambda j: (0, j))] + [ANYWHERE] * len(after),
        out_specs=pl.BlockSpec((HALF, GROUP, rows), lambda j: (0, j, 0)),
        out_shape=jax.ShapeDtypeStruct((HALF, CHI, rows), BF16),
        compiler_params=params(),
        cost_estimate=cost(1),
        name="k_major",
    )(x, *after)


def k_minor(parts, after):
    rows = parts[0].shape[2]
    n_parts = len(parts)

    def kernel(*refs):
        whole = jnp.concatenate([ref[...] for ref in refs[:n_parts]], axis=0)
        refs[-1][...] = jnp.transpose(whole, (1, 0, 2)).reshape(GROUP * HALF, rows).T

    return pl.pallas_call(
        kernel,
        grid=(CHI // GROUP,),
        in_specs=[pl.BlockSpec((x.shape[0], GROUP, rows), lambda j: (0, j, 0)) for x in parts]
        + [ANYWHERE] * len(after),
        out_specs=pl.BlockSpec((rows, GROUP * HALF), lambda j: (0, j)),
        out_shape=jax.ShapeDtypeStruct((rows, CHI * HALF), BF16),
        compiler_params=params(),
        cost_estimate=cost(1),
        name="k_minor",
    )(*parts, *after)


def held_back(arrays, after):
    n_arrays = len(arrays)
    return pl.pallas_call(
        lambda *refs: None,
        in_specs=[ANYWHERE] * (n_arrays + len(after)),
        out_specs=[ANYWHERE] * n_arrays,
        out_shape=[jax.ShapeDtypeStruct(x.shape, x.dtype) for x in arrays],
        input_output_aliases={j: j for j in range(n_arrays)},
        compiler_params=pltpu.CompilerParams(vmem_limit_bytes=VMEM_MIB * MIB),
        cost_estimate=cost(1),
        name="held_back",
    )(*arrays, *after)


def absorbed_chunk(me, lower, corner_t, ds, first, count, after):
    rows = lower.shape[2]
    n_out = len(ds)

    def kernel(me_ref, l_ref, *refs):
        c_refs, outs = refs[:n_out], refs[-n_out:]
        low = l_ref[0]
        for c_ref, out in zip(c_refs, outs):
            out[0] = nn(c_ref[...], low).astype(BF16)

    def corner_spec(d):
        return pl.BlockSpec((rows, CHI), lambda k, me: (me[0] ^ d, 0))

    return pl.pallas_call(
        kernel,
        grid_spec=pltpu.PrefetchScalarGridSpec(
            num_scalar_prefetch=1,
            grid=(count,),
            in_specs=[pl.BlockSpec((1, CHI, rows), lambda k, me: (first + k, 0, 0))]
            + [corner_spec(d) for d in ds] + [ANYWHERE] * len(after),
            out_specs=[pl.BlockSpec((1, rows, rows), lambda k, me: (k, 0, 0))] * n_out,
        ),
        out_shape=[jax.ShapeDtypeStruct((count, rows, rows), BF16)] * n_out,
        compiler_params=params(),
        cost_estimate=cost(count),
        name="absorbed",
    )(me, lower, *[corner_t] * n_out, *after)


def half_chunk(me, blocks, lower, corner, held, first, count, after):
    rows = lower.shape[2]
    n = CHI // rows
    step = 2
    n_held = 0 if held is None else 2

    def kernel(me_ref, l_ref, *refs):
        f_refs, c_refs = refs[:n], refs[n:2 * n]
        half_ref, corner_ref, pair_ref = refs[-3:]

        @pl.when(pl.program_id(0) == 0)
        def _():
            if n_held:
                corner_ref[...] = refs[-5][...]
                pair_ref[...] = refs[-4][...]
            else:
                corner_ref[...] = jnp.zeros_like(corner_ref)
                pair_ref[...] = jnp.zeros_like(pair_ref)

        for j in range(step):
            total = nn(c_refs[0][...], f_refs[0][j])
            for d in range(1, n):
                total += nn(c_refs[d][...], f_refs[d][j])
            half_ref[j] = total.astype(BF16)
            part = total * l_ref[j].astype(F32)
            pair_ref[...] += jnp.sum(part.reshape(CHI // 8, 8, rows), axis=0)
        low = jnp.concatenate([l_ref[j] for j in range(step)], axis=1)
        for d in range(n):
            full = jnp.concatenate([f_refs[d][j] for j in range(step)], axis=1)
            place = pl.ds(pl.multiple_of((me_ref[0] ^ d) * rows, rows), rows)
            corner_ref[:, place] += nt(low, full)

    def corner_spec(d):
        return pl.BlockSpec((CHI, rows), lambda k, me: (0, me[0] ^ d))

    def block_spec(offset):
        return pl.BlockSpec((step, rows, rows), lambda k, me: (offset // step + k, 0, 0))

    corner_sum = pl.BlockSpec((CHI, CHI), lambda k, me: (0, 0))
    pair_sum = pl.BlockSpec((8, rows), lambda k, me: (0, 0))
    operands = [me, lower, *[x for x, _ in blocks], *[corner] * n, *after]
    operands += held if n_held else []
    return pl.pallas_call(
        kernel,
        grid_spec=pltpu.PrefetchScalarGridSpec(
            num_scalar_prefetch=1,
            grid=(count // step,),
            in_specs=[pl.BlockSpec((step, CHI, rows), lambda k, me: (first // step + k, 0, 0))]
            + [block_spec(offset) for _, offset in blocks]
            + [corner_spec(d) for d in range(n)] + [ANYWHERE] * len(after)
            + [corner_sum, pair_sum][:n_held],
            out_specs=[
                pl.BlockSpec((step, CHI, rows), lambda k, me: (k, 0, 0)),
                corner_sum,
                pair_sum,
            ],
        ),
        out_shape=[
            jax.ShapeDtypeStruct((count, CHI, rows), BF16),
            jax.ShapeDtypeStruct((CHI, CHI), F32),
            jax.ShapeDtypeStruct((8, rows), F32),
        ],
        compiler_params=params(),
        cost_estimate=cost(2 * count),
        name="grad_half",
    )(*operands)


def edge_chunk(blocks, grad_blocks, held, first, count, after):
    rows = blocks[0][0].shape[1]
    n = CHI // rows
    has_held = held is not None

    def kernel(*refs):
        a_refs, g_refs, out = refs[:n], refs[n:2 * n], refs[-1]
        total = nn(a_refs[0][0], g_refs[0][...])
        for d in range(1, n):
            total += nn(a_refs[d][0], g_refs[d][...])
        out[...] = total.astype(BF16)

    def block_spec(offset):
        return pl.BlockSpec((1, rows, rows), lambda k: (offset + k, 0, 0))

    operands = [*[x for x, _ in blocks], *grad_blocks, *after]
    operands += [held] if has_held else []
    return pl.pallas_call(
        kernel,
        grid=(count,),
        in_specs=[block_spec(offset) for _, offset in blocks]
        + [pl.BlockSpec((rows, CHI), lambda k: (0, 0))] * n
        + [ANYWHERE] * (len(after) + has_held),
        out_specs=pl.BlockSpec((rows, CHI), lambda k: (0, first + k)),
        out_shape=jax.ShapeDtypeStruct((rows, HALF * CHI), BF16),
        input_output_aliases={len(operands) - 1: 0} if has_held else {},
        compiler_params=params(),
        cost_estimate=cost(count),
        name="grad_edge",
    )(*operands)


def exchanged(blocks):
    far_first = {d: swapped(blocks[d], d) for d in reversed(range(1, len(blocks)))}
    return [blocks[0]] + [far_first[d] for d in range(1, len(blocks))]


def same_charge(rows_ref, columns_ref, x):
    return jnp.where(rows_ref[...] == columns_ref[...], x, 0.0)


def masked_corner(corner, row_charge, column_charge, after):
    rows = CHI // ENV

    def kernel(x_ref, r_ref, c_ref, *refs):
        masked = same_charge(r_ref, c_ref, x_ref[...].astype(F32)).astype(BF16)
        refs[-2][...] = masked
        refs[-1][...] = masked.T

    return pl.pallas_call(
        kernel,
        grid=(ENV,),
        in_specs=[
            pl.BlockSpec((rows, CHI), lambda j: (j, 0)),
            pl.BlockSpec((rows, 1), lambda j: (j, 0)),
            pl.BlockSpec((1, CHI), lambda j: (0, 0)),
        ] + [ANYWHERE] * len(after),
        out_specs=[
            pl.BlockSpec((rows, CHI), lambda j: (j, 0)),
            pl.BlockSpec((CHI, rows), lambda j: (0, j)),
        ],
        out_shape=[jax.ShapeDtypeStruct((CHI, CHI), BF16)] * 2,
        compiler_params=params(),
        cost_estimate=cost(1),
        name="near_corner",
    )(corner, row_charge, column_charge, *after)


def corner_halves(me, total, after):
    rows = CHI // ENV

    def kernel(me_ref, total_ref, *refs):
        refs[-1][0] = total_ref[...].astype(BF16)

    return pl.pallas_call(
        kernel,
        grid_spec=pltpu.PrefetchScalarGridSpec(
            num_scalar_prefetch=1,
            grid=(2,),
            in_specs=[pl.BlockSpec((rows, CHI), lambda h, me: (2 * h + 1 - me[0] % 2, 0))]
            + [ANYWHERE] * len(after),
            out_specs=pl.BlockSpec((1, rows, CHI), lambda h, me: (h, 0, 0)),
        ),
        out_shape=jax.ShapeDtypeStruct((2, rows, CHI), BF16),
        compiler_params=params(),
        cost_estimate=cost(1),
        name="corner_halves",
    )(me, total, *after)


def corner_quarter(me, total, halves, after):
    rows = CHI // ENV

    def kernel(me_ref, total_ref, half_ref, *refs):
        refs[-1][...] = (total_ref[...] + half_ref[0].astype(F32)).astype(BF16)

    return pl.pallas_call(
        kernel,
        grid_spec=pltpu.PrefetchScalarGridSpec(
            num_scalar_prefetch=1,
            grid=(1,),
            in_specs=[
                pl.BlockSpec((rows, CHI), lambda q, me: (me[0] ^ 2, 0)),
                pl.BlockSpec((1, rows, CHI), lambda q, me: ((me[0] ^ 2) // 2, 0, 0)),
            ] + [ANYWHERE] * len(after),
            out_specs=pl.BlockSpec((rows, CHI), lambda q, me: (0, 0)),
        ),
        out_shape=jax.ShapeDtypeStruct((rows, CHI), BF16),
        compiler_params=params(),
        cost_estimate=cost(1),
        name="corner_quarter",
    )(me, total, halves, *after)


def corner_rows(me, total, halves, quarter, charges, after):
    rows = CHI // ENV

    def kernel(me_ref, total_ref, half_ref, quarter_ref, r_ref, c_ref, *refs):
        whole = total_ref[...] + half_ref[0].astype(F32) + quarter_ref[...].astype(F32)
        refs[-1][...] = same_charge(r_ref, c_ref, whole).astype(BF16)

    return pl.pallas_call(
        kernel,
        grid_spec=pltpu.PrefetchScalarGridSpec(
            num_scalar_prefetch=1,
            grid=(1,),
            in_specs=[
                pl.BlockSpec((rows, CHI), lambda q, me: (me[0], 0)),
                pl.BlockSpec((1, rows, CHI), lambda q, me: (me[0] // 2, 0, 0)),
                pl.BlockSpec((rows, CHI), lambda q, me: (0, 0)),
                pl.BlockSpec((rows, 1), lambda q, me: (me[0], 0)),
                pl.BlockSpec((1, CHI), lambda q, me: (0, 0)),
            ] + [ANYWHERE] * len(after),
            out_specs=pl.BlockSpec((rows, CHI), lambda q, me: (0, 0)),
        ),
        out_shape=jax.ShapeDtypeStruct((rows, CHI), BF16),
        compiler_params=params(),
        cost_estimate=cost(1),
        name="grad_corner",
    )(me, total, halves, quarter, *charges, *after)


def charge_masks(parity):
    charges = jnp.repeat(parity, BLK, axis=1)
    corner_mask = charges[0][:, None] == charges[1][None, :]
    out_mask = charges[2][:, None] == charges[3][None, :]
    return corner_mask, out_mask


def spans(counts):
    return [(sum(counts[:j]), count) for j, count in enumerate(counts)]


def chunked_shards(corner, top_edge, half_system, values, cotangent, parity):
    rows = CHI // ENV
    me = lax.axis_index("env").astype(jnp.int32)
    me_arr = me.reshape(1)
    near_corner = row_major(corner_moved(row_major(corner[0, 0]), 1))
    above = jnp.repeat(passed_along(parity[0, 0], "row", 1), BLK, axis=1)
    row_charge, column_charge = above[0][:, None], above[1][None, :]
    top, half = top_edge[0, 0], half_system[0, 0]
    full_spans, edge_spans = spans(FULL_CHUNKS), spans(EDGE_CHUNKS)

    full, edge_far, edge_near, half_parts = {}, {}, [], []
    totals = halves = quarter = grad_corner = grad_edge = grad_half = None
    last = []
    for step in ORDER.split():
        what, j = step[0], int(step[1:] or 0)
        if what == "F":
            if j == 0:
                grad_blocks, blocks = first_full_chunk(
                    me_arr, parity[0, 0], top, values[0], cotangent[0, 0],
                    (3, 2, 1, 0), full_spans[0][1],
                )
            else:
                blocks = full_chunk(top, grad_blocks, (3, 2, 1, 0), *full_spans[j], last)
            last = [blocks[0]]
            if j in HELD_BACK:
                blocks = held_back(blocks, [full[j - 1][d] for d in HELD_BACK[j]] + [near_corner] * CORNER_FIRST)
                last = [blocks[0]]
            full[j] = [swapped(x, 3 - d, 1) for d, x in enumerate(blocks)][::-1]
        elif what == "C":
            near_corner, corner_t = masked_corner(near_corner, row_charge, column_charge, last)
            last = [corner_t]
        elif what == "T":
            lower = k_major(half, last)
            last = [lower]
        elif what == "A":
            blocks = absorbed_chunk(me_arr, lower, corner_t, (3, 2), *edge_spans[j], last)
            last = [blocks[0]]
            edge_far[j] = [swapped(blocks[0], 3, -1), swapped(blocks[1], 2, -1)]
        elif what == "a":
            blocks = absorbed_chunk(me_arr, lower, corner_t, (0, 1), 0, HALF, last)
            last = [blocks[0]]
            edge_near = [swapped(blocks[0], 0, -1), swapped(blocks[1], 1, -1)]
        elif what == "H":
            first, count = full_spans[j]
            blocks = [(x, 0) for x in full[j]]
            part, *totals = half_chunk(
                me_arr, blocks, lower, near_corner, totals, first, count, last
            )
            last = [totals[1]]
            half_parts.append(part)
        elif what == "M":
            grad_half = k_minor(half_parts, last)
            last = [grad_half]
        elif what == "R" and j == 1:
            halves = corner_halves(me_arr, totals[0], last)
            last = [halves]
            halves = swapped(halves, 1)
        elif what == "R" and j == 2:
            quarter = corner_quarter(me_arr, totals[0], halves, last)
            last = [quarter]
            quarter = swapped(quarter, 2)
        elif what == "R" and j == 3:
            charged = (row_charge, column_charge)
            grad_corner = corner_rows(me_arr, totals[0], halves, quarter, charged, last)
            last = [grad_corner]
            grad_corner = corner_moved(grad_corner, -1)
        elif what == "R":
            last = last + [grad_corner]
        elif what == "W":
            last = last + full[j]
        elif what == "w":
            last = last + full[j][:2]
        elif what == "E":
            first, count = edge_spans[j]
            blocks = [(x, first) for x in edge_near] + [(x, 0) for x in reversed(edge_far[j])]
            grad_edge = edge_chunk(
                blocks, grad_blocks, grad_edge, first, count,
                [x for x in last if x is not grad_edge],
            )
            last = [grad_edge]
    own_values = lax.dynamic_slice_in_dim(values[0, 0], me * rows, rows, 0)
    pair_sums = passed_along(jnp.sum(totals[1], axis=0), "row", -1)
    grad_values = -0.5 * pair_sums / own_values

    return (
        grad_corner[None, None],
        grad_edge[None, None],
        grad_half[None, None],
        grad_values[None, None],
    )


def whole_shards(corner, top_edge, half_system, values, cotangent, parity):
    rows = top_edge.shape[2]
    row_start = lax.axis_index("env") * rows
    corner_mask, out_mask = charge_masks(parity[0, 0])
    near_corner = passed_along(corner[0, 0], "col", 1)
    near_corner = jnp.where(corner_mask, near_corner, jnp.zeros_like(near_corner))
    lower_half = passed_along(half_system[0, 0], "row", -1).reshape(rows, CHI, HALF)
    absorbed = jnp.einsum("ab,iak->ibk", near_corner, lower_half, preferred_element_type=F32)
    absorbed = absorbed.astype(BF16).reshape(rows, CHI * HALF)
    gathered = lax.all_to_all(absorbed, "env", split_axis=1, concat_axis=0, tiled=True)
    edge_mat = top_edge[0, 0].reshape(rows * HALF, CHI)
    grad_new = jnp.where(
        out_mask, values[0, 0][:, None] ** (-0.5) * cotangent[0, 0].astype(F32), 0.0
    ).astype(BF16)
    grad_edge = jnp.einsum("ij,ie->je", gathered, grad_new, preferred_element_type=F32)
    grad_edge = grad_edge.astype(BF16).reshape(rows, HALF * CHI)
    grad_full = jnp.einsum("ie,je->ij", grad_new, edge_mat, preferred_element_type=F32)
    totals = lax.psum(jnp.sum(gathered * grad_full, axis=1), "env")
    pair_sums = lax.dynamic_slice_in_dim(totals, row_start, rows, 0)
    own_values = lax.dynamic_slice_in_dim(values[0, 0], row_start, rows, 0)
    grad_values = -0.5 * pair_sums / own_values
    grad_back = lax.all_to_all(
        grad_full.astype(BF16), "env", split_axis=0, concat_axis=1, tiled=True
    ).reshape(rows, CHI, HALF)
    grad_half = jnp.einsum("ab,ibk->iak", near_corner, grad_back, preferred_element_type=F32)
    grad_half = grad_half.astype(BF16).reshape(rows, CHI * HALF)
    summed = jnp.einsum("iak,ibk->ab", lower_half, grad_back, preferred_element_type=F32)
    summed = lax.psum_scatter(summed, "env", scatter_dimension=0, tiled=True)
    own_mask = lax.dynamic_slice_in_dim(corner_mask, row_start, rows, 0)
    grad_corner = jnp.where(own_mask, summed, 0.0).astype(BF16)
    grad_corner = passed_along(grad_corner, "col", -1)
    grad_half = passed_along(grad_half, "row", 1)
    return (
        grad_corner[None, None],
        grad_edge[None, None],
        grad_half[None, None],
        grad_values[None, None],
    )


def solution(mesh):
    chunked = mesh.shape["env"] == ENV
    return jax.shard_map(
        chunked_shards if chunked else whole_shards,
        mesh=mesh,
        in_specs=(
            P("row", "col", None, None),
            P("row", "col", "env", None),
            P("row", "col", "env", None),
            P("row", "col", None),
            P("row", "col", None, None),
            P("row", "col", None, None),
        ),
        out_specs=(
            P("row", "col", "env", None),
            P("row", "col", "env", None),
            P("row", "col", "env", None),
            P("row", "col", "env"),
        ),
        check_vma=False,
    )
```

```python
import functools

import jax
import jax.numpy as jnp
from jax import lax
from jax.experimental import pallas as pl
from jax.experimental.layout import Layout, with_layout_constraint
from jax.experimental.pallas import tpu as pltpu
from jax.sharding import PartitionSpec as P

CHI = 1024
HALF = 32
BLK = 128

FULL_CHUNKS = (4, 28)
EDGE_CHUNKS = (9, 9, 6, 4, 3, 1)
ENV = 4

MIB = 1 << 20
VMEM_MIB = 56
COST_BITS = 20
CORNER_FIRST = 1
HELD_BACK = {1: (2, 3)}
ORDER = "F0 F1 C T A0 a A1 H0 H1 R1 A2 E0 A3 R2 M E1 A4 R3 E2 A5 E3 R4 E4 E5"
F32 = jnp.float32
BF16 = jnp.bfloat16


def passed_along(x, axis, by):
    size = lax.axis_size(axis)
    return lax.ppermute(x, axis, [(i, (i + by) % size) for i in range(size)])


def swapped(x, d, rows_on=0):
    n_row, n_env = lax.axis_size("row"), lax.axis_size("env")
    if not rows_on:
        return lax.ppermute(x, "env", [(i, i ^ d) for i in range(n_env)])
    pairs = [
        (r * n_env + i, (r + rows_on) % n_row * n_env + (i ^ d))
        for r in range(n_row) for i in range(n_env)
    ]
    return lax.ppermute(x, ("row", "env"), pairs)


def corner_moved(x, by):
    n_row, n_col = lax.axis_size("row"), lax.axis_size("col")
    pairs = [
        (r * n_col + c, (r + by) % n_row * n_col + (c + by) % n_col)
        for r in range(n_row) for c in range(n_col)
    ]
    return lax.ppermute(x, ("row", "col"), pairs)


def nn(a, b):
    return jnp.dot(a, b, preferred_element_type=F32)


def nt(a, b):
    return lax.dot_general(a, b, (((1,), (1,)), ((), ())), preferred_element_type=F32)


ANYWHERE = pl.BlockSpec(memory_space=pl.ANY)


def params(dims=1):
    return pltpu.CompilerParams(
        vmem_limit_bytes=VMEM_MIB * MIB, dimension_semantics=("arbitrary",) * dims
    )


def cost(count):
    return pl.CostEstimate(
        flops=count << COST_BITS, bytes_accessed=count << (COST_BITS - 8), transcendentals=0
    )


def row_major(x):
    return with_layout_constraint(x, Layout(tuple(range(x.ndim))))


def full_chunk(top_edge, grad_blocks, ds, first, count, after):
    rows = top_edge.shape[0]
    n_out = len(ds)
    step = 2 if first % 2 == 0 and count % 2 == 0 else 1

    def kernel(t_ref, *refs):
        g_refs, outs = refs[:n_out], refs[-n_out:]
        t = jnp.concatenate([t_ref[:, j * CHI:(j + 1) * CHI] for j in range(step)], axis=0)
        for g_ref, out in zip(g_refs, outs):
            out[...] = nt(t, g_ref[...]).astype(BF16).reshape(step, rows, rows)

    return pl.pallas_call(
        kernel,
        grid=(count // step,),
        in_specs=[pl.BlockSpec((rows, step * CHI), lambda k: (0, first // step + k))]
        + [pl.BlockSpec((rows, CHI), lambda k: (0, 0))] * n_out + [ANYWHERE] * len(after),
        out_specs=[pl.BlockSpec((step, rows, rows), lambda k: (k, 0, 0))] * n_out,
        out_shape=[jax.ShapeDtypeStruct((count, rows, rows), BF16)] * n_out,
        compiler_params=params(),
        cost_estimate=cost(count),
        name="grad_full",
    )(top_edge, *[grad_blocks[d] for d in ds], *after)


def first_full_chunk(me, parity, top_edge, values, cotangent, ds, count, after):
    rows = top_edge.shape[0]
    n = len(ds)
    step = 2 if count % 2 == 0 else 1

    def kernel(me_ref, parity_ref, t_ref, *refs):
        v_refs, cot_refs = refs[:n], refs[n:2 * n]
        g_refs, outs = refs[-2 * n:-n], refs[-n:]

        @pl.when(pl.program_id(0) == 0)
        def _():
            for d, v_ref, cot_ref, g_ref in zip(ds, v_refs, cot_refs, g_refs):
                weight = jnp.broadcast_to(v_ref[...], (8, rows)).T[:, :1] ** (-0.5)
                for i in range(rows // BLK):
                    charge = parity_ref[2, (me_ref[0] ^ d) * (rows // BLK) + i]
                    part = slice(i * BLK, (i + 1) * BLK)
                    for e in range(CHI // BLK):
                        across = slice(e * BLK, (e + 1) * BLK)
                        scaled = weight[part] * cot_ref[part, across].astype(F32)
                        kept = jnp.where(charge == parity_ref[3, e], scaled, 0.0)
                        g_ref[part, across] = kept.astype(BF16)

        t = jnp.concatenate([t_ref[:, j * CHI:(j + 1) * CHI] for j in range(step)], axis=0)
        for g_ref, out in zip(g_refs, outs):
            out[...] = nt(t, g_ref[...]).astype(BF16).reshape(step, rows, rows)

    def value_spec(d):
        return pl.BlockSpec((1, rows), lambda k, me, parity: (0, me[0] ^ d))

    def cotangent_spec(d):
        return pl.BlockSpec((rows, CHI), lambda k, me, parity: (me[0] ^ d, 0))

    made = pl.pallas_call(
        kernel,
        grid_spec=pltpu.PrefetchScalarGridSpec(
            num_scalar_prefetch=2,
            grid=(count // step,),
            in_specs=[pl.BlockSpec((rows, step * CHI), lambda k, me, parity: (0, k))]
            + [value_spec(d) for d in ds] + [cotangent_spec(d) for d in ds]
            + [ANYWHERE] * len(after),
            out_specs=[pl.BlockSpec((rows, CHI), lambda k, me, parity: (0, 0))] * n
            + [pl.BlockSpec((step, rows, rows), lambda k, me, parity: (k, 0, 0))] * n,
        ),
        out_shape=[jax.ShapeDtypeStruct((rows, CHI), BF16)] * n
        + [jax.ShapeDtypeStruct((count, rows, rows), BF16)] * n,
        compiler_params=params(),
        cost_estimate=cost(count),
        name="grad_full",
    )(me, parity, top_edge, *[values] * n, *[cotangent] * n, *after)
    return made[:n], made[n:]


GROUP = 64


def k_major(x, after):
    rows = x.shape[0]

    def kernel(x_ref, *refs):
        turned = x_ref[...].T.reshape(GROUP, HALF, rows)
        refs[-1][...] = jnp.transpose(turned, (1, 0, 2))

    return pl.pallas_call(
        kernel,
        grid=(CHI // GROUP,),
        in_specs=[pl.BlockSpec((rows, GROUP * HALF), lambda j: (0, j))] + [ANYWHERE] * len(after),
        out_specs=pl.BlockSpec((HALF, GROUP, rows), lambda j: (0, j, 0)),
        out_shape=jax.ShapeDtypeStruct((HALF, CHI, rows), BF16),
        compiler_params=params(),
        cost_estimate=cost(1),
        name="k_major",
    )(x, *after)


def k_minor(parts, after):
    rows = parts[0].shape[2]
    n_parts = len(parts)

    def kernel(*refs):
        whole = jnp.concatenate([ref[...] for ref in refs[:n_parts]], axis=0)
        refs[-1][...] = jnp.transpose(whole, (1, 0, 2)).reshape(GROUP * HALF, rows).T

    return pl.pallas_call(
        kernel,
        grid=(CHI // GROUP,),
        in_specs=[pl.BlockSpec((x.shape[0], GROUP, rows), lambda j: (0, j, 0)) for x in parts]
        + [ANYWHERE] * len(after),
        out_specs=pl.BlockSpec((rows, GROUP * HALF), lambda j: (0, j)),
        out_shape=jax.ShapeDtypeStruct((rows, CHI * HALF), BF16),
        compiler_params=params(),
        cost_estimate=cost(1),
        name="k_minor",
    )(*parts, *after)


def held_back(arrays, after):
    n_arrays = len(arrays)
    return pl.pallas_call(
        lambda *refs: None,
        in_specs=[ANYWHERE] * (n_arrays + len(after)),
        out_specs=[ANYWHERE] * n_arrays,
        out_shape=[jax.ShapeDtypeStruct(x.shape, x.dtype) for x in arrays],
        input_output_aliases={j: j for j in range(n_arrays)},
        compiler_params=pltpu.CompilerParams(vmem_limit_bytes=VMEM_MIB * MIB),
        cost_estimate=cost(1),
        name="held_back",
    )(*arrays, *after)


def absorbed_chunk(me, lower, corner_t, ds, first, count, after):
    rows = lower.shape[2]
    n_out = len(ds)

    def kernel(me_ref, l_ref, *refs):
        c_refs, outs = refs[:n_out], refs[-n_out:]
        low = l_ref[0]
        for c_ref, out in zip(c_refs, outs):
            out[0] = nn(c_ref[...], low).astype(BF16)

    def corner_spec(d):
        return pl.BlockSpec((rows, CHI), lambda k, me: (me[0] ^ d, 0))

    return pl.pallas_call(
        kernel,
        grid_spec=pltpu.PrefetchScalarGridSpec(
            num_scalar_prefetch=1,
            grid=(count,),
            in_specs=[pl.BlockSpec((1, CHI, rows), lambda k, me: (first + k, 0, 0))]
            + [corner_spec(d) for d in ds] + [ANYWHERE] * len(after),
            out_specs=[pl.BlockSpec((1, rows, rows), lambda k, me: (k, 0, 0))] * n_out,
        ),
        out_shape=[jax.ShapeDtypeStruct((count, rows, rows), BF16)] * n_out,
        compiler_params=params(),
        cost_estimate=cost(count),
        name="absorbed",
    )(me, lower, *[corner_t] * n_out, *after)


def half_chunk(me, blocks, lower, corner, held, first, count, after):
    rows = lower.shape[2]
    n = CHI // rows
    step = 2
    n_held = 0 if held is None else 2

    def kernel(me_ref, l_ref, *refs):
        f_refs, c_refs = refs[:n], refs[n:2 * n]
        half_ref, corner_ref, pair_ref = refs[-3:]

        @pl.when(pl.program_id(0) == 0)
        def _():
            if n_held:
                corner_ref[...] = refs[-5][...]
                pair_ref[...] = refs[-4][...]
            else:
                corner_ref[...] = jnp.zeros_like(corner_ref)
                pair_ref[...] = jnp.zeros_like(pair_ref)

        for j in range(step):
            total = nn(c_refs[0][...], f_refs[0][j])
            for d in range(1, n):
                total += nn(c_refs[d][...], f_refs[d][j])
            half_ref[j] = total.astype(BF16)
            part = total * l_ref[j].astype(F32)
            pair_ref[...] += jnp.sum(part.reshape(CHI // 8, 8, rows), axis=0)
        low = jnp.concatenate([l_ref[j] for j in range(step)], axis=1)
        for d in range(n):
            full = jnp.concatenate([f_refs[d][j] for j in range(step)], axis=1)
            place = pl.ds(pl.multiple_of((me_ref[0] ^ d) * rows, rows), rows)
            corner_ref[:, place] += nt(low, full)

    def corner_spec(d):
        return pl.BlockSpec((CHI, rows), lambda k, me: (0, me[0] ^ d))

    def block_spec(offset):
        return pl.BlockSpec((step, rows, rows), lambda k, me: (offset // step + k, 0, 0))

    corner_sum = pl.BlockSpec((CHI, CHI), lambda k, me: (0, 0))
    pair_sum = pl.BlockSpec((8, rows), lambda k, me: (0, 0))
    operands = [me, lower, *[x for x, _ in blocks], *[corner] * n, *after]
    operands += held if n_held else []
    return pl.pallas_call(
        kernel,
        grid_spec=pltpu.PrefetchScalarGridSpec(
            num_scalar_prefetch=1,
            grid=(count // step,),
            in_specs=[pl.BlockSpec((step, CHI, rows), lambda k, me: (first // step + k, 0, 0))]
            + [block_spec(offset) for _, offset in blocks]
            + [corner_spec(d) for d in range(n)] + [ANYWHERE] * len(after)
            + [corner_sum, pair_sum][:n_held],
            out_specs=[
                pl.BlockSpec((step, CHI, rows), lambda k, me: (k, 0, 0)),
                corner_sum,
                pair_sum,
            ],
        ),
        out_shape=[
            jax.ShapeDtypeStruct((count, CHI, rows), BF16),
            jax.ShapeDtypeStruct((CHI, CHI), F32),
            jax.ShapeDtypeStruct((8, rows), F32),
        ],
        compiler_params=params(),
        cost_estimate=cost(2 * count),
        name="grad_half",
    )(*operands)


def edge_chunk(blocks, grad_blocks, held, first, count, after):
    rows = blocks[0][0].shape[1]
    n = CHI // rows
    has_held = held is not None

    def kernel(*refs):
        a_refs, g_refs, out = refs[:n], refs[n:2 * n], refs[-1]
        total = nn(a_refs[0][0], g_refs[0][...])
        for d in range(1, n):
            total += nn(a_refs[d][0], g_refs[d][...])
        out[...] = total.astype(BF16)

    def block_spec(offset):
        return pl.BlockSpec((1, rows, rows), lambda k: (offset + k, 0, 0))

    operands = [*[x for x, _ in blocks], *grad_blocks, *after]
    operands += [held] if has_held else []
    return pl.pallas_call(
        kernel,
        grid=(count,),
        in_specs=[block_spec(offset) for _, offset in blocks]
        + [pl.BlockSpec((rows, CHI), lambda k: (0, 0))] * n
        + [ANYWHERE] * (len(after) + has_held),
        out_specs=pl.BlockSpec((rows, CHI), lambda k: (0, first + k)),
        out_shape=jax.ShapeDtypeStruct((rows, HALF * CHI), BF16),
        input_output_aliases={len(operands) - 1: 0} if has_held else {},
        compiler_params=params(),
        cost_estimate=cost(count),
        name="grad_edge",
    )(*operands)


def exchanged(blocks):
    far_first = {d: swapped(blocks[d], d) for d in reversed(range(1, len(blocks)))}
    return [blocks[0]] + [far_first[d] for d in range(1, len(blocks))]


def same_charge(rows_ref, columns_ref, x):
    return jnp.where(rows_ref[...] == columns_ref[...], x, 0.0)


def masked_corner(corner, row_charge, column_charge, after):
    rows = CHI // ENV

    def kernel(x_ref, r_ref, c_ref, *refs):
        masked = same_charge(r_ref, c_ref, x_ref[...].astype(F32)).astype(BF16)
        refs[-2][...] = masked
        refs[-1][...] = masked.T

    return pl.pallas_call(
        kernel,
        grid=(ENV,),
        in_specs=[
            pl.BlockSpec((rows, CHI), lambda j: (j, 0)),
            pl.BlockSpec((rows, 1), lambda j: (j, 0)),
            pl.BlockSpec((1, CHI), lambda j: (0, 0)),
        ] + [ANYWHERE] * len(after),
        out_specs=[
            pl.BlockSpec((rows, CHI), lambda j: (j, 0)),
            pl.BlockSpec((CHI, rows), lambda j: (0, j)),
        ],
        out_shape=[jax.ShapeDtypeStruct((CHI, CHI), BF16)] * 2,
        compiler_params=params(),
        cost_estimate=cost(1),
        name="near_corner",
    )(corner, row_charge, column_charge, *after)


def corner_halves(me, total, after):
    rows = CHI // ENV

    def kernel(me_ref, total_ref, *refs):
        refs[-1][0] = total_ref[...].astype(BF16)

    return pl.pallas_call(
        kernel,
        grid_spec=pltpu.PrefetchScalarGridSpec(
            num_scalar_prefetch=1,
            grid=(2,),
            in_specs=[pl.BlockSpec((rows, CHI), lambda h, me: (2 * h + 1 - me[0] % 2, 0))]
            + [ANYWHERE] * len(after),
            out_specs=pl.BlockSpec((1, rows, CHI), lambda h, me: (h, 0, 0)),
        ),
        out_shape=jax.ShapeDtypeStruct((2, rows, CHI), BF16),
        compiler_params=params(),
        cost_estimate=cost(1),
        name="corner_halves",
    )(me, total, *after)


def corner_quarter(me, total, halves, after):
    rows = CHI // ENV

    def kernel(me_ref, total_ref, half_ref, *refs):
        refs[-1][...] = (total_ref[...] + half_ref[0].astype(F32)).astype(BF16)

    return pl.pallas_call(
        kernel,
        grid_spec=pltpu.PrefetchScalarGridSpec(
            num_scalar_prefetch=1,
            grid=(1,),
            in_specs=[
                pl.BlockSpec((rows, CHI), lambda q, me: (me[0] ^ 2, 0)),
                pl.BlockSpec((1, rows, CHI), lambda q, me: ((me[0] ^ 2) // 2, 0, 0)),
            ] + [ANYWHERE] * len(after),
            out_specs=pl.BlockSpec((rows, CHI), lambda q, me: (0, 0)),
        ),
        out_shape=jax.ShapeDtypeStruct((rows, CHI), BF16),
        compiler_params=params(),
        cost_estimate=cost(1),
        name="corner_quarter",
    )(me, total, halves, *after)


def corner_rows(me, total, halves, quarter, charges, after):
    rows = CHI // ENV

    def kernel(me_ref, total_ref, half_ref, quarter_ref, r_ref, c_ref, *refs):
        whole = total_ref[...] + half_ref[0].astype(F32) + quarter_ref[...].astype(F32)
        refs[-1][...] = same_charge(r_ref, c_ref, whole).astype(BF16)

    return pl.pallas_call(
        kernel,
        grid_spec=pltpu.PrefetchScalarGridSpec(
            num_scalar_prefetch=1,
            grid=(1,),
            in_specs=[
                pl.BlockSpec((rows, CHI), lambda q, me: (me[0], 0)),
                pl.BlockSpec((1, rows, CHI), lambda q, me: (me[0] // 2, 0, 0)),
                pl.BlockSpec((rows, CHI), lambda q, me: (0, 0)),
                pl.BlockSpec((rows, 1), lambda q, me: (me[0], 0)),
                pl.BlockSpec((1, CHI), lambda q, me: (0, 0)),
            ] + [ANYWHERE] * len(after),
            out_specs=pl.BlockSpec((rows, CHI), lambda q, me: (0, 0)),
        ),
        out_shape=jax.ShapeDtypeStruct((rows, CHI), BF16),
        compiler_params=params(),
        cost_estimate=cost(1),
        name="grad_corner",
    )(me, total, halves, quarter, *charges, *after)


def charge_masks(parity):
    charges = jnp.repeat(parity, BLK, axis=1)
    corner_mask = charges[0][:, None] == charges[1][None, :]
    out_mask = charges[2][:, None] == charges[3][None, :]
    return corner_mask, out_mask


def spans(counts):
    return [(sum(counts[:j]), count) for j, count in enumerate(counts)]


def chunked_shards(corner, top_edge, half_system, values, cotangent, parity):
    rows = CHI // ENV
    me = lax.axis_index("env").astype(jnp.int32)
    me_arr = me.reshape(1)
    near_corner = row_major(corner_moved(row_major(corner[0, 0]), 1))
    above = jnp.repeat(passed_along(parity[0, 0], "row", 1), BLK, axis=1)
    row_charge, column_charge = above[0][:, None], above[1][None, :]
    top, half = top_edge[0, 0], half_system[0, 0]
    full_spans, edge_spans = spans(FULL_CHUNKS), spans(EDGE_CHUNKS)

    full, edge_far, edge_near, half_parts = {}, {}, [], []
    totals = halves = quarter = grad_corner = grad_edge = grad_half = None
    last = []
    for step in ORDER.split():
        what, j = step[0], int(step[1:] or 0)
        if what == "F":
            if j == 0:
                def first_blocks(ds, after):
                    return first_full_chunk(
                        me_arr, parity[0, 0], top, values[0], cotangent[0, 0],
                        ds, full_spans[0][1], after,
                    )

                far_grad, far = first_blocks((3, 2), last)
                near_grad, near = first_blocks((1, 0), [far[0]])
                grad_blocks, blocks = [*far_grad, *near_grad][::-1], [*far, *near]
                last = [near[0]]
            else:
                blocks = full_chunk(top, grad_blocks, (3, 2, 1, 0), *full_spans[j], last)
                last = [blocks[0]]
            if j in HELD_BACK:
                blocks = held_back(blocks, [full[j - 1][d] for d in HELD_BACK[j]] + [near_corner] * CORNER_FIRST)
                last = [blocks[0]]
            full[j] = [swapped(x, 3 - d, 1) for d, x in enumerate(blocks)][::-1]
        elif what == "C":
            near_corner, corner_t = masked_corner(near_corner, row_charge, column_charge, last)
            last = [corner_t]
        elif what == "T":
            lower = k_major(half, last)
            last = [lower]
        elif what == "A":
            blocks = absorbed_chunk(me_arr, lower, corner_t, (3, 2), *edge_spans[j], last)
            last = [blocks[0]]
            edge_far[j] = [swapped(blocks[0], 3, -1), swapped(blocks[1], 2, -1)]
        elif what == "a":
            blocks = absorbed_chunk(me_arr, lower, corner_t, (0, 1), 0, HALF, last)
            last = [blocks[0]]
            edge_near = [swapped(blocks[0], 0, -1), swapped(blocks[1], 1, -1)]
        elif what == "H":
            first, count = full_spans[j]
            blocks = [(x, 0) for x in full[j]]
            part, *totals = half_chunk(
                me_arr, blocks, lower, near_corner, totals, first, count, last
            )
            last = [totals[1]]
            half_parts.append(part)
        elif what == "M":
            grad_half = k_minor(half_parts, last)
            last = [grad_half]
        elif what == "R" and j == 1:
            halves = corner_halves(me_arr, totals[0], last)
            last = [halves]
            halves = swapped(halves, 1)
        elif what == "R" and j == 2:
            quarter = corner_quarter(me_arr, totals[0], halves, last)
            last = [quarter]
            quarter = swapped(quarter, 2)
        elif what == "R" and j == 3:
            charged = (row_charge, column_charge)
            grad_corner = corner_rows(me_arr, totals[0], halves, quarter, charged, last)
            last = [grad_corner]
            grad_corner = corner_moved(grad_corner, -1)
        elif what == "R":
            last = last + [grad_corner]
        elif what == "W":
            last = last + full[j]
        elif what == "w":
            last = last + full[j][:2]
        elif what == "E":
            first, count = edge_spans[j]
            blocks = [(x, first) for x in edge_near] + [(x, 0) for x in reversed(edge_far[j])]
            grad_edge = edge_chunk(
                blocks, grad_blocks, grad_edge, first, count,
                [x for x in last if x is not grad_edge],
            )
            last = [grad_edge]
    own_values = lax.dynamic_slice_in_dim(values[0, 0], me * rows, rows, 0)
    pair_sums = passed_along(jnp.sum(totals[1], axis=0), "row", -1)
    grad_values = -0.5 * pair_sums / own_values

    return (
        grad_corner[None, None],
        grad_edge[None, None],
        grad_half[None, None],
        grad_values[None, None],
    )


def whole_shards(corner, top_edge, half_system, values, cotangent, parity):
    rows = top_edge.shape[2]
    row_start = lax.axis_index("env") * rows
    corner_mask, out_mask = charge_masks(parity[0, 0])
    near_corner = passed_along(corner[0, 0], "col", 1)
    near_corner = jnp.where(corner_mask, near_corner, jnp.zeros_like(near_corner))
    lower_half = passed_along(half_system[0, 0], "row", -1).reshape(rows, CHI, HALF)
    absorbed = jnp.einsum("ab,iak->ibk", near_corner, lower_half, preferred_element_type=F32)
    absorbed = absorbed.astype(BF16).reshape(rows, CHI * HALF)
    gathered = lax.all_to_all(absorbed, "env", split_axis=1, concat_axis=0, tiled=True)
    edge_mat = top_edge[0, 0].reshape(rows * HALF, CHI)
    grad_new = jnp.where(
        out_mask, values[0, 0][:, None] ** (-0.5) * cotangent[0, 0].astype(F32), 0.0
    ).astype(BF16)
    grad_edge = jnp.einsum("ij,ie->je", gathered, grad_new, preferred_element_type=F32)
    grad_edge = grad_edge.astype(BF16).reshape(rows, HALF * CHI)
    grad_full = jnp.einsum("ie,je->ij", grad_new, edge_mat, preferred_element_type=F32)
    totals = lax.psum(jnp.sum(gathered * grad_full, axis=1), "env")
    pair_sums = lax.dynamic_slice_in_dim(totals, row_start, rows, 0)
    own_values = lax.dynamic_slice_in_dim(values[0, 0], row_start, rows, 0)
    grad_values = -0.5 * pair_sums / own_values
    grad_back = lax.all_to_all(
        grad_full.astype(BF16), "env", split_axis=0, concat_axis=1, tiled=True
    ).reshape(rows, CHI, HALF)
    grad_half = jnp.einsum("ab,ibk->iak", near_corner, grad_back, preferred_element_type=F32)
    grad_half = grad_half.astype(BF16).reshape(rows, CHI * HALF)
    summed = jnp.einsum("iak,ibk->ab", lower_half, grad_back, preferred_element_type=F32)
    summed = lax.psum_scatter(summed, "env", scatter_dimension=0, tiled=True)
    own_mask = lax.dynamic_slice_in_dim(corner_mask, row_start, rows, 0)
    grad_corner = jnp.where(own_mask, summed, 0.0).astype(BF16)
    grad_corner = passed_along(grad_corner, "col", -1)
    grad_half = passed_along(grad_half, "row", 1)
    return (
        grad_corner[None, None],
        grad_edge[None, None],
        grad_half[None, None],
        grad_values[None, None],
    )


def solution(mesh):
    chunked = mesh.shape["env"] == ENV
    return jax.shard_map(
        chunked_shards if chunked else whole_shards,
        mesh=mesh,
        in_specs=(
            P("row", "col", None, None),
            P("row", "col", "env", None),
            P("row", "col", "env", None),
            P("row", "col", None),
            P("row", "col", None, None),
            P("row", "col", None, None),
        ),
        out_specs=(
            P("row", "col", "env", None),
            P("row", "col", "env", None),
            P("row", "col", "env", None),
            P("row", "col", "env"),
        ),
        check_vma=False,
    )
```
